32 devices in a mesh: rep: 8 (over y, x, core), shard: 4 (over z).
Axes of the slice: x: 2, y: 2, z: 4, core: 2. Of those that a mesh axis runs over, the one named last changes fastest.
Arguments:
- tokens: bfloat16 [160, 197, 768], P(('rep', 'shard')), may hold values from -6 to 6
- counts: int32 [32], P(('rep', 'shard')), may hold values from 4 to 5, as said below
- w_qkv: bfloat16 [768, 2304], P('shard'), may hold values from -0.21875 to 0.21875
- b_query: bfloat16 [768], P('shard'), may hold values from -3 to 3
- b_value: bfloat16 [768], P('shard'), may hold values from -3 to 3
- w_proj: bfloat16 [768, 768], P('shard'), may hold values from -0.625 to 0.625
- b_proj: bfloat16 [768], P('shard'), may hold values from -3 to 3
- gain_one: bfloat16 [768], P('shard'), may hold values from 0.5 to 1.5
- bias_one: bfloat16 [768], P('shard'), may hold values from -2 to 2
- gain_two: bfloat16 [768], P('shard'), may hold values from 0.5 to 1.5
- bias_two: bfloat16 [768], P('shard'), may hold values from -2 to 2
- w_up: bfloat16 [768, 3072], P('shard'), may hold values from -0.21875 to 0.21875
- b_up: bfloat16 [3072], P('shard'), may hold values from -3 to 3
- w_down: bfloat16 [3072, 768], P('shard'), may hold values from -0.109375 to 0.109375
- b_down: bfloat16 [768], P('shard'), may hold values from -3 to 3
- out_grad: bfloat16 [160, 197, 768], P(('rep', 'shard')), may hold values from -6 to 6
Outputs:
- layer_out: bfloat16 [160, 197, 768], P(('rep', 'shard'))
- grad_tokens: bfloat16 [160, 197, 768], P(('rep', 'shard'))
- grad_w_qkv: float32 [768, 2304], P('shard')
- grad_b_query: float32 [768], P('shard')
- grad_b_value: float32 [768], P('shard')
- grad_w_proj: float32 [768, 768], P('shard')
- grad_b_proj: float32 [768], P('shard')
- grad_gain_one: float32 [768], P('shard')
- grad_bias_one: float32 [768], P('shard')
- grad_gain_two: float32 [768], P('shard')
- grad_bias_two: float32 [768], P('shard')
- grad_w_up: float32 [768, 3072], P('shard')
- grad_b_up: float32 [3072], P('shard')
- grad_w_down: float32 [3072, 768], P('shard')
- grad_b_down: float32 [768], P('shard')
The draws below stay inside these ranges and needn't reach their ends.
Inputs may be any that keep to these rules, and one draw needn't show every extreme that they name: Device d holds images in its first counts[d] slots; in every draw some device holds 5 and some 4.
All inputs are finite; a program needn't handle non-finite values.
Results may differ from the reference program's by a relative error of at most 0.015.
Values may be sent and summed in bfloat16 or wider, within the bound.
No kernel may reach another device: no remote copies, remote signals or barrier semaphores. Data moves between devices by JAX's collectives and lax.ppermute only.
A program may use at most 192 MiB of HBM per device.

```python
import jax
import jax.numpy as jnp
from jax import lax

D = 768
H = 12
HD = 64
FF = 3072
LEN = 197
SLOTS = 5
SLOTS_ALL = 160


def draw_counts(key, part):
    key = jax.random.fold_in(key, 7)
    device_total = SLOTS_ALL // SLOTS
    draw_key, pick_key = jax.random.split(key)
    extra_one = jax.random.randint(draw_key, (device_total,), 0, 2)
    shuffled = jax.random.permutation(pick_key, device_total)
    extra_one = extra_one.at[shuffled[0]].set(1).at[shuffled[1]].set(0)
    return (extra_one + SLOTS - 1).astype(jnp.int32)


def shard_levels(key, dims, cuts, smallest, largest):
    def one(dim, blocks):
        draws = jax.random.uniform(jax.random.fold_in(jax.random.fold_in(key, 6), dim), (blocks,), jnp.float32, smallest / len(cuts), largest / len(cuts))
        return jnp.repeat(jnp.exp(draws), dims[dim] // blocks).reshape((-1,) + (1,) * (len(dims) - dim - 1))

    level = one(*cuts[0])
    for cut in cuts[1:]:
        level = level * one(*cut)
    return level


def normal_values(stream_key, dims, spread, limit, cuts=(), kind=jnp.bfloat16):
    level = shard_levels(stream_key, dims, cuts, -0.22, 0.18) if cuts else 1.0
    array = jax.random.normal(stream_key, dims, jnp.float32) * spread * level
    return jnp.minimum(jnp.maximum(array, -limit), limit).astype(kind)


def setup_inputs(seed: int = 0) -> dict:
    keys = jax.random.split(jax.random.key(seed), 17)
    return {
        "tokens": normal_values(keys[0], (SLOTS_ALL, LEN, D), 1.0, 6.0, ((0, 32),)),
        "counts": draw_counts(jax.random.fold_in(keys[16], 71), 0),
        "w_qkv": normal_values(keys[2], (D, 3 * D), D ** -0.5, 0.21875, ((0, 4),)),
        "b_query": normal_values(keys[3], (D,), 0.5, 3.0, ((0, 4),)),
        "b_value": normal_values(keys[4], (D,), 0.5, 3.0, ((0, 4),)),
        "w_proj": normal_values(keys[5], (D, D), (D // 8) ** -0.5, 0.625, ((0, 4),)),
        "b_proj": normal_values(keys[6], (D,), 0.5, 3.0, ((0, 4),)),
        "gain_one": jnp.clip(1.0 + 0.1 * jax.random.normal(keys[7], (D,), jnp.float32), 0.5, 1.5).astype(jnp.bfloat16),
        "bias_one": normal_values(keys[8], (D,), 0.3, 2.0, ((0, 4),)),
        "gain_two": jnp.clip(1.0 + 0.1 * jax.random.normal(keys[9], (D,), jnp.float32), 0.5, 1.5).astype(jnp.bfloat16),
        "bias_two": normal_values(keys[10], (D,), 0.3, 2.0, ((0, 4),)),
        "w_up": normal_values(keys[11], (D, FF), D ** -0.5, 0.21875, ((0, 4),)),
        "b_up": normal_values(keys[12], (FF,), 0.5, 3.0, ((0, 4),)),
        "w_down": normal_values(keys[13], (FF, D), FF ** -0.5, 0.109375, ((0, 4),)),
        "b_down": normal_values(keys[14], (D,), 0.5, 3.0, ((0, 4),)),
        "out_grad": normal_values(keys[15], (SLOTS_ALL, LEN, D), 1.0, 6.0, ((0, 32),)),
    }


@jax.custom_vjp
def low(v):
    return lax.optimization_barrier(v.astype(jnp.bfloat16)).astype(jnp.float32)

@jax.custom_vjp
def low_back(v):
    return v

def low_keep(v):
    return (low(v), None)

def low_pass(kept, grad):
    return (grad,)

def back_keep(v):
    return (v, None)

def back_low(kept, grad):
    return (low(grad),)
low.defvjp(low_keep, low_pass)
low_back.defvjp(back_keep, back_low)
EPSILON = 1e-06

def normalize(values_in, gain_in, shift_in):
    row_mean = lax.optimization_barrier(jnp.mean(values_in, axis=-1, keepdims=True))
    centred = values_in - row_mean
    row_var = lax.optimization_barrier(jnp.mean(centred * centred, axis=-1, keepdims=True))
    return centred * lax.rsqrt(row_var + EPSILON) * gain_in + shift_in

def block_forward(inputs, params):
    w_qkv, b_query, b_value, w_proj, b_proj, gain_one, bias_one, gain_two, bias_two, w_up, b_up, w_down, b_down = params
    highest = lax.Precision.HIGHEST
    slot_count = inputs.shape[0] // LEN
    normed_one = low(normalize(inputs, gain_one, bias_one))
    joined = jnp.dot(normed_one, w_qkv, precision=highest)
    joined = joined + jnp.concatenate([b_query, jnp.zeros_like(b_query), b_value])
    joined = low(low_back(joined))
    split_heads = joined.reshape(slot_count, LEN, 3, H, HD)
    queries = split_heads[:, :, 0]
    key_part = split_heads[:, :, 1]
    value_part = split_heads[:, :, 2]
    scores = jnp.einsum('bqhd,bkhd->bhqk', queries, key_part, precision=highest) * HD ** (-0.5)
    scores = low_back(scores)
    shifted = scores - lax.optimization_barrier(jnp.max(scores, axis=-1, keepdims=True))
    expo = jnp.exp(shifted)
    attention = expo / lax.optimization_barrier(jnp.sum(expo, axis=-1, keepdims=True))
    mixed_heads = jnp.einsum('bhqk,bkhd->bqhd', low(attention), value_part, precision=highest)
    mixed_heads = low(low_back(mixed_heads.reshape(-1, D)))
    attended = low_back(jnp.dot(mixed_heads, w_proj, precision=highest) + b_proj)
    middle = inputs + attended
    normed_two = low(normalize(middle, gain_two, bias_two))
    hidden = low_back(jnp.dot(normed_two, w_up, precision=highest) + b_up)
    active = low(jax.nn.gelu(hidden, approximate=False))
    return middle + low_back(jnp.dot(active, w_down, precision=highest) + b_down)

def reference(tokens, counts, w_qkv, b_query, b_value, w_proj, b_proj, gain_one, bias_one, gain_two, bias_two, w_up, b_up, w_down, b_down, out_grad):
    params = tuple((item.astype(jnp.float32) for item in (w_qkv, b_query, b_value, w_proj, b_proj, gain_one, bias_one, gain_two, bias_two, w_up, b_up, w_down, b_down)))
    device_total = counts.shape[0]
    token_blocks = tokens.reshape(device_total, SLOTS * LEN, D)
    grad_blocks = out_grad.reshape(device_total, SLOTS * LEN, D)
    slot_live = jnp.arange(SLOTS, dtype=jnp.int32)[None, :] < counts[:, None]
    row_live = jnp.repeat(slot_live, LEN, axis=1).astype(jnp.float32)[..., None]

    def device_step(totals, block):
        token_rows, cotangent, live_rows = block
        result, pullback = jax.vjp(block_forward, token_rows.astype(jnp.float32), params)
        back_rows, back_params = pullback(cotangent.astype(jnp.float32) * live_rows)
        totals = jax.tree.map(jnp.add, totals, back_params)
        return (totals, ((result * live_rows).astype(jnp.bfloat16), back_rows.astype(jnp.bfloat16)))
    zero_grads = jax.tree.map(jnp.zeros_like, params)
    totals, (outputs, backs) = lax.scan(device_step, zero_grads, (token_blocks, grad_blocks, row_live))
    return (outputs.reshape(tokens.shape), backs.reshape(tokens.shape), totals[0], totals[1], totals[2], totals[3], totals[4], totals[5], totals[6], totals[7], totals[8], totals[9], totals[10], totals[11], totals[12])
```

```python
import functools
import math

import jax
import jax.numpy as jnp
from jax import lax
from jax.experimental import pallas as pl
from jax.experimental.pallas import tpu as pltpu
from jax.sharding import Mesh, PartitionSpec as P

H = 12
HD = 64
EPSILON = 1e-06
ROOT_HALF = 1.0 / math.sqrt(2.0)
INV_ROOT_TAU = 1.0 / math.sqrt(2.0 * math.pi)
f32 = jnp.float32
bf16 = jnp.bfloat16
SWAP = [(0, 1), (1, 0)]


def norm_parts(values_in):
    row_mean = jnp.mean(values_in, axis=-1, keepdims=True)
    centred = values_in - row_mean
    inverse = lax.rsqrt(jnp.mean(centred * centred, axis=-1, keepdims=True) + EPSILON)
    return (centred * inverse, inverse)


def norm_back(grad_normal, normal_rows, inverse_rows):
    first_mean = jnp.mean(grad_normal, axis=-1, keepdims=True)
    second_mean = jnp.mean(grad_normal * normal_rows, axis=-1, keepdims=True)
    return inverse_rows * (grad_normal - first_mean - normal_rows * second_mean)


def dot_nt(a, b):
    return lax.dot_general(a, b, (((1,), (1,)), ((), ())), preferred_element_type=f32)


def dot_tn(a, b):
    return lax.dot_general(a, b, (((0,), (0,)), ((), ())), preferred_element_type=f32)


def dot_nn(a, b):
    return jnp.dot(a, b, preferred_element_type=f32)


def attention_kernel(length, qkv_ref, out_ref, prob_ref):
    rows = qkv_ref.shape[1]
    width = H * HD
    first = lax.broadcasted_iota(jnp.int32, (1, 2 * HD), 1) < HD
    key_live = lax.broadcasted_iota(jnp.int32, (rows, 1), 0) < length
    for pair in range(H // 2):
        lanes = pl.ds(pair * 2 * HD, 2 * HD)
        q2 = qkv_ref[0, :, pl.ds(pair * 2 * HD, 2 * HD)] * jnp.asarray(HD ** (-0.5), bf16)
        k2 = qkv_ref[0, :, pl.ds(width + pair * 2 * HD, 2 * HD)]
        v2 = qkv_ref[0, :, pl.ds(2 * width + pair * 2 * HD, 2 * HD)]
        total = None
        for half in range(2):
            mask = first if half == 0 else jnp.logical_not(first)
            scores = dot_nt(jnp.where(mask, k2, jnp.zeros_like(k2)), q2)
            scores = jnp.where(key_live, scores, -1e30)
            expo = jnp.exp(scores - jnp.max(scores, axis=0, keepdims=True))
            probs = (expo * (1.0 / jnp.sum(expo, axis=0, keepdims=True))).astype(bf16)
            prob_ref[0, 2 * pair + half] = probs
            part = dot_tn(probs, jnp.where(mask, v2, jnp.zeros_like(v2)))
            total = part if total is None else total + part
        out_ref[0, :, lanes] = total.astype(bf16)


def attention_back_kernel(qkv_ref, prob_ref, grad_ref, out_ref, sums_ref):
    width = H * HD
    first = lax.broadcasted_iota(jnp.int32, (1, 2 * HD), 1) < HD
    scale = jnp.asarray(HD ** (-0.5), f32)

    @pl.when(pl.program_id(0) == 0)
    def _():
        sums_ref[...] = jnp.zeros_like(sums_ref)

    for pair in range(H // 2):
        spots = [pl.ds(part * width + pair * 2 * HD, 2 * HD) for part in range(3)]
        q2 = qkv_ref[0, :, spots[0]]
        k2 = qkv_ref[0, :, spots[1]]
        v2 = qkv_ref[0, :, spots[2]]
        g2 = grad_ref[0, :, spots[0]]
        totals = [None, None, None]
        for half in range(2):
            mask = first if half == 0 else jnp.logical_not(first)

            def keep(v):
                return jnp.where(mask, v, jnp.zeros_like(v))

            probs = prob_ref[0, 2 * pair + half]
            g_half = keep(g2)
            grad_probs = dot_nt(v2, g_half)
            probs_wide = probs.astype(f32)
            delta = jnp.sum(grad_probs * probs_wide, axis=0, keepdims=True)
            grad_scores = (probs_wide * (grad_probs - delta)).astype(bf16)
            parts = (
                dot_tn(grad_scores, keep(k2)),
                dot_nn(grad_scores, keep(q2)),
                dot_nn(probs, g_half),
            )
            totals = [p if t is None else t + p for t, p in zip(totals, parts)]
        for part in range(3):
            value = totals[part] if part == 2 else totals[part] * scale
            value = value.astype(bf16)
            out_ref[0, :, spots[part]] = value
            sums_ref[:, spots[part]] += jnp.sum(value.astype(f32), axis=0, keepdims=True)


def attention(qkv, length):
    slots, rows, wide = qkv.shape
    width = wide // 3
    return pl.pallas_call(
        functools.partial(attention_kernel, length),
        grid=(slots,),
        in_specs=[pl.BlockSpec((1, rows, wide), lambda i: (i, 0, 0))],
        out_specs=[
            pl.BlockSpec((1, rows, width), lambda i: (i, 0, 0)),
            pl.BlockSpec((1, H, rows, rows), lambda i: (i, 0, 0, 0)),
        ],
        out_shape=[
            jax.ShapeDtypeStruct((slots, rows, width), bf16),
            jax.ShapeDtypeStruct((slots, H, rows, rows), bf16),
        ],
        compiler_params=pltpu.CompilerParams(vmem_limit_bytes=28 * 2**20),
        cost_estimate=pl.CostEstimate(
            flops=slots * H * 4 * rows * rows * 256, bytes_accessed=30000000, transcendentals=0
        ),
        name="attention",
    )(qkv)


def attention_back(qkv, probs, grad):
    slots, rows, wide = qkv.shape
    width = wide // 3
    return pl.pallas_call(
        attention_back_kernel,
        grid=(slots,),
        in_specs=[
            pl.BlockSpec((1, rows, wide), lambda i: (i, 0, 0)),
            pl.BlockSpec((1, H, rows, rows), lambda i: (i, 0, 0, 0)),
            pl.BlockSpec((1, rows, width), lambda i: (i, 0, 0)),
        ],
        out_specs=[
            pl.BlockSpec((1, rows, wide), lambda i: (i, 0, 0)),
            pl.BlockSpec((1, wide), lambda i: (0, 0)),
        ],
        out_shape=[
            jax.ShapeDtypeStruct((slots, rows, wide), bf16),
            jax.ShapeDtypeStruct((1, wide), f32),
        ],
        compiler_params=pltpu.CompilerParams(vmem_limit_bytes=28 * 2**20),
        cost_estimate=pl.CostEstimate(
            flops=slots * H * 8 * rows * rows * 256, bytes_accessed=60000000, transcendentals=0
        ),
        name="attention_back",
    )(qkv, probs, grad)


class Net:
    def __init__(self, rep_bits, shard_bits):
        self.core, self.x, self.y = rep_bits[-1], rep_bits[-2], rep_bits[-3]
        self.extra = tuple(rep_bits[:-3])
        self.rep = tuple(rep_bits)
        self.shard = tuple(shard_bits)
        self.dims = self.shard + (self.x, self.y)
        self.bit = {name: lax.axis_index(name) for name in self.rep + self.shard}

    def place(self, mine, other, name, spot):
        bit = self.bit[name]
        low = jnp.where(bit == 0, mine, other)
        high = jnp.where(bit == 0, other, mine)
        return low, high, spot

    def grow(self, piece, have, name):
        other = lax.ppermute(piece, name, SWAP)
        have = tuple(d for d in self.dims if d in have or d == name)
        low, high, spot = self.place(piece, other, name, have.index(name))
        return jnp.stack([low, high], axis=spot), have

    def halve(self, piece, have, name):
        spot = have.index(name)
        bit = self.bit[name]
        send = lax.dynamic_index_in_dim(piece, 1 - bit, spot, keepdims=False)
        keep = lax.dynamic_index_in_dim(piece, bit, spot, keepdims=False)
        other = lax.ppermute(send, name, SWAP)
        piece = (keep.astype(f32) + other.astype(f32)).astype(bf16)
        return piece, tuple(d for d in have if d != name)

    def gather(self, weight, streams):
        rows, columns = weight.shape
        half, fine = columns // 2, rows // 4
        mine = lax.dynamic_slice_in_dim(weight, self.bit[self.core] * half, half, 1)
        mine = mine.reshape(2, 2, fine, half)
        mine = lax.dynamic_index_in_dim(mine, self.bit[self.x], 0, keepdims=False)
        mine = lax.dynamic_index_in_dim(mine, self.bit[self.y], 0, keepdims=False)
        done = []
        for start, stop, order in streams(self, half):
            piece, have = mine[:, start:stop], ()
            for name in order:
                piece, have = self.grow(piece, have, name)
            other = lax.ppermute(piece, self.core, SWAP)
            low, high, _ = self.place(piece, other, self.core, None)
            done.append((low, high))
        full = jnp.concatenate([d[0] for d in done] + [d[1] for d in done], axis=-1)
        return full.reshape(-1, columns)

    def reduce(self, left, right, streams):
        columns = right.shape[1]
        half = columns // 2
        core = self.bit[self.core]
        send = lax.dynamic_slice_in_dim(right, (1 - core) * half, half, 1)
        keep = lax.dynamic_slice_in_dim(right, core * half, half, 1)
        other = lax.ppermute(dot_tn(left, send).astype(bf16), self.core, SWAP)
        total = (dot_tn(left, keep) + other.astype(f32)).astype(bf16)
        count = len(self.dims)
        total = total.reshape((2,) * count + (-1, half))
        done = []
        for start, stop, order in streams(self, half):
            piece, have = total[..., start:stop], self.dims
            for name in order:
                piece, have = self.halve(piece, have, name)
            for name in self.extra:
                piece = (piece.astype(f32) + lax.ppermute(piece, name, SWAP).astype(f32)).astype(bf16)
            have = ()
            for name in reversed([n for n in order if n in (self.x, self.y)]):
                piece, have = self.grow(piece, have, name)
            other = lax.ppermute(piece, self.core, SWAP)
            low, high, _ = self.place(piece, other, self.core, None)
            done.append((low, high))
        full = jnp.concatenate([d[0] for d in done] + [d[1] for d in done], axis=-1)
        return full.reshape(-1, columns).astype(f32)

    def rotations(self, pick):
        count = 2 ** len(self.shard)
        got = [pick(0)]
        for k in range(1, count):
            got.append(
                lax.ppermute(pick(k), self.shard, [(i, (i + k) % count) for i in range(count)])
            )
        return got

    def place_in_group(self):
        me = 0
        for name in self.shard:
            me = 2 * me + self.bit[name]
        return me

    def gather_small(self, small):
        got = jnp.stack(self.rotations(lambda k: small))
        count = got.shape[0]
        me = self.place_in_group()
        rows = [
            lax.dynamic_index_in_dim(got, (me + count - s) % count, 0, keepdims=False)
            for s in range(count)
        ]
        return jnp.stack(rows)

    def reduce_small(self, values):
        count = values.shape[0]
        me = self.place_in_group()
        got = self.rotations(
            lambda k: lax.dynamic_index_in_dim(values, (me + k) % count, 0, keepdims=False)
        )
        total = functools.reduce(jnp.add, got)
        for name in reversed(self.rep):
            total = total + lax.ppermute(total, name, SWAP)
        return total


def both_ways(net, half):
    cut = (half // 256) * 128
    z = net.shard
    return [(0, cut, z + (net.x, net.y)), (cut, half, z + (net.y, net.x))]


def x_way(net, half):
    return [(0, half, net.shard + (net.x, net.y))]


def y_way(net, half):
    return [(0, half, net.shard + (net.y, net.x))]


def down_along(net, half):
    return [(0, half, net.shard[::-1] + (net.x, net.y))]


def down_across(net, half):
    return [(0, half, (net.x, net.y) + net.shard[::-1])]


def down_across_y(net, half):
    return [(0, half, (net.y, net.x) + net.shard[::-1])]


def down_both(net, half):
    cut = (half // 256) * 128
    z = net.shard[::-1]
    return [(0, cut, z + (net.x, net.y)), (cut, half, (net.y, net.x) + z)]


def per_device(
    rep_bits,
    shard_bits,
    tokens,
    counts,
    w_qkv,
    b_query,
    b_value,
    w_proj,
    b_proj,
    gain_one,
    bias_one,
    gain_two,
    bias_two,
    w_up,
    b_up,
    w_down,
    b_down,
    out_grad,
):
    net = Net(rep_bits, shard_bits)
    group = 2 ** len(shard_bits)
    slot_count, length, width = tokens.shape
    padded = -(-length // 16) * 16
    row_count = slot_count * padded
    wide = w_up.shape[1]
    part = width // group
    fill = ((0, 0), (0, padded - length), (0, 0))

    small = jnp.stack(
        [b_query, b_value, b_proj, gain_one, bias_one, gain_two, bias_two, b_down]
    )
    small = jnp.concatenate([small, b_up.reshape(-1, part)], axis=0)
    small = net.gather_small(small).astype(f32)
    rows = small[:, :8].transpose(1, 0, 2).reshape(8, width)
    query_bias, value_bias, proj_bias, gain_1, bias_1, gain_2, bias_2, down_bias = (
        rows[i] for i in range(8)
    )
    up_bias = small[:, 8:].reshape(wide)

    qkv_full = net.gather(w_qkv, both_ways)
    proj_full = net.gather(w_proj, x_way)
    up_full = net.gather(w_up, x_way)
    down_full = net.gather(w_down, y_way)

    live_slots = (jnp.arange(slot_count, dtype=jnp.int32) < counts[0]).astype(f32)
    live_rows = jnp.repeat(live_slots, padded)[:, None]
    inputs = jnp.pad(tokens, fill).reshape(row_count, width).astype(f32)
    normal_one, inverse_one = norm_parts(inputs)
    normed_one = (normal_one * gain_1 + bias_1).astype(bf16)
    qkv_bias = jnp.concatenate([query_bias, jnp.zeros_like(query_bias), value_bias])
    joined = (dot_nn(normed_one, qkv_full) + qkv_bias).astype(bf16)
    joined = joined.reshape(slot_count, padded, 3 * width)
    mixed, probs = attention(joined, length)
    mixed = mixed.reshape(row_count, width)
    middle = inputs + (dot_nn(mixed, proj_full) + proj_bias)
    normal_two, inverse_two = norm_parts(middle)
    normed_two = (normal_two * gain_2 + bias_2).astype(bf16)
    hidden = dot_nn(normed_two, up_full) + up_bias
    share = 0.5 * (1.0 + lax.erf(hidden * ROOT_HALF))
    active = (hidden * share).astype(bf16)
    slope = (share + hidden * jnp.exp(-0.5 * hidden * hidden) * INV_ROOT_TAU).astype(bf16)
    result = middle + (dot_nn(active, down_full) + down_bias)
    layer_out = (result * live_rows).astype(bf16)
    layer_out = layer_out.reshape(slot_count, padded, width)[:, :length]

    grad_branch = jnp.pad(out_grad, fill).reshape(row_count, width)
    grad_branch = grad_branch * live_rows.astype(bf16)
    grad_down_b = jnp.sum(grad_branch.astype(f32), axis=0)
    grad_down_w = net.reduce(active, grad_branch, down_along)
    grad_active = dot_nt(grad_branch, down_full)
    grad_hidden = (grad_active * slope.astype(f32)).astype(bf16)
    grad_up_b = jnp.sum(grad_hidden.astype(f32), axis=0)
    grad_up_w = net.reduce(normed_two, grad_hidden, down_across)
    grad_normed_two = dot_nt(grad_hidden, up_full)
    grad_gain_two = jnp.sum(grad_normed_two * normal_two, axis=0)
    grad_bias_two = jnp.sum(grad_normed_two, axis=0)
    grad_middle = grad_branch.astype(f32) + norm_back(
        grad_normed_two * gain_2, normal_two, inverse_two
    )
    grad_attn = grad_middle.astype(bf16)
    grad_proj_b = jnp.sum(grad_attn.astype(f32), axis=0)
    grad_proj_w = net.reduce(mixed, grad_attn, down_across_y)
    grad_mixed = dot_nt(grad_attn, proj_full).astype(bf16)
    grad_joined, joined_sums = attention_back(
        joined, probs, grad_mixed.reshape(slot_count, padded, width)
    )
    grad_joined = grad_joined.reshape(row_count, 3 * width)
    grad_query_b = joined_sums[0, :width]
    grad_value_b = joined_sums[0, 2 * width :]
    grad_qkv_w = net.reduce(normed_one, grad_joined, down_both)
    grad_normed_one = dot_nt(grad_joined, qkv_full)
    grad_gain_one = jnp.sum(grad_normed_one * normal_one, axis=0)
    grad_bias_one = jnp.sum(grad_normed_one, axis=0)
    grad_inputs = grad_middle + norm_back(grad_normed_one * gain_1, normal_one, inverse_one)
    grad_tokens = grad_inputs.astype(bf16).reshape(slot_count, padded, width)[:, :length]

    def by_owner(vectors):
        return jnp.stack(vectors).reshape(len(vectors), group, -1).transpose(1, 0, 2)

    early = by_owner([grad_proj_b, grad_gain_two, grad_bias_two, grad_down_b])
    early_up = grad_up_b.reshape(group, -1, part)
    early = net.reduce_small(jnp.concatenate([early, early_up], axis=1))
    late = net.reduce_small(by_owner([grad_query_b, grad_value_b, grad_gain_one, grad_bias_one]))
    return (
        layer_out,
        grad_tokens,
        grad_qkv_w,
        late[0],
        late[1],
        grad_proj_w,
        early[0],
        late[2],
        late[3],
        early[1],
        early[2],
        grad_up_w,
        early[4:].reshape(-1),
        grad_down_w,
        early[3],
    )


def solution(mesh):
    rep, shard = mesh.shape["rep"], mesh.shape["shard"]
    rep_bits = tuple(f"r{i}" for i in range(rep.bit_length() - 1))
    shard_bits = tuple(f"s{i}" for i in range(shard.bit_length() - 1))
    fine = Mesh(mesh.devices.reshape((2,) * (len(rep_bits) + len(shard_bits))), rep_bits + shard_bits)
    every = P(rep_bits + shard_bits, None, None)
    matrix = P(shard_bits, None)
    vector = P(shard_bits)
    return jax.shard_map(
        functools.partial(per_device, rep_bits, shard_bits),
        mesh=fine,
        in_specs=(
            every,
            P(rep_bits + shard_bits),
            matrix,
            vector,
            vector,
            matrix,
            vector,
            vector,
            vector,
            vector,
            vector,
            matrix,
            vector,
            matrix,
            vector,
            every,
        ),
        out_specs=(
            every,
            every,
            matrix,
            vector,
            vector,
            matrix,
            vector,
            vector,
            vector,
            vector,
            vector,
            matrix,
            vector,
            matrix,
            vector,
        ),
        check_vma=False,
    )
```

```python
import functools
import math

import jax
import jax.numpy as jnp
from jax import lax
from jax.experimental import pallas as pl
from jax.experimental.pallas import tpu as pltpu
from jax.sharding import Mesh, PartitionSpec as P

H = 12
HD = 64
EPSILON = 1e-06
ROOT_HALF = 1.0 / math.sqrt(2.0)
INV_ROOT_TAU = 1.0 / math.sqrt(2.0 * math.pi)
f32 = jnp.float32
bf16 = jnp.bfloat16
SWAP = [(0, 1), (1, 0)]
FREE = pl.CostEstimate(flops=0, bytes_accessed=0, transcendentals=0)


def norm_parts(values_in):
    row_mean = jnp.mean(values_in, axis=-1, keepdims=True)
    centred = values_in - row_mean
    inverse = lax.rsqrt(jnp.mean(centred * centred, axis=-1, keepdims=True) + EPSILON)
    return (centred * inverse, inverse)


def norm_back(grad_normal, normal_rows, inverse_rows):
    first_mean = jnp.mean(grad_normal, axis=-1, keepdims=True)
    second_mean = jnp.mean(grad_normal * normal_rows, axis=-1, keepdims=True)
    return inverse_rows * (grad_normal - first_mean - normal_rows * second_mean)


def dot_nt(a, b):
    return lax.dot_general(a, b, (((1,), (1,)), ((), ())), preferred_element_type=f32)


def dot_tn(a, b):
    return lax.dot_general(a, b, (((0,), (0,)), ((), ())), preferred_element_type=f32)


def dot_nn(a, b):
    return jnp.dot(a, b, preferred_element_type=f32)


def attention_kernel(length, qkv_ref, out_ref, prob_ref):
    rows = qkv_ref.shape[1]
    width = H * HD
    first = lax.broadcasted_iota(jnp.int32, (1, 2 * HD), 1) < HD
    key_live = lax.broadcasted_iota(jnp.int32, (rows, 1), 0) < length
    for pair in range(H // 2):
        lanes = pl.ds(pair * 2 * HD, 2 * HD)
        q2 = qkv_ref[0, :, pl.ds(pair * 2 * HD, 2 * HD)] * jnp.asarray(HD ** (-0.5), bf16)
        k2 = qkv_ref[0, :, pl.ds(width + pair * 2 * HD, 2 * HD)]
        v2 = qkv_ref[0, :, pl.ds(2 * width + pair * 2 * HD, 2 * HD)]
        total = None
        for half in range(2):
            mask = first if half == 0 else jnp.logical_not(first)
            scores = dot_nt(jnp.where(mask, k2, jnp.zeros_like(k2)), q2)
            scores = jnp.where(key_live, scores, -1e30)
            expo = jnp.exp(scores - jnp.max(scores, axis=0, keepdims=True))
            probs = (expo * (1.0 / jnp.sum(expo, axis=0, keepdims=True))).astype(bf16)
            prob_ref[0, 2 * pair + half] = probs
            part = dot_tn(probs, jnp.where(mask, v2, jnp.zeros_like(v2)))
            total = part if total is None else total + part
        out_ref[0, :, lanes] = total.astype(bf16)


def attention_back_kernel(qkv_ref, prob_ref, grad_ref, out_ref, sums_ref):
    width = H * HD
    first = lax.broadcasted_iota(jnp.int32, (1, 2 * HD), 1) < HD
    scale = jnp.asarray(HD ** (-0.5), f32)

    @pl.when(pl.program_id(0) == 0)
    def _():
        sums_ref[...] = jnp.zeros_like(sums_ref)

    for pair in range(H // 2):
        spots = [pl.ds(part * width + pair * 2 * HD, 2 * HD) for part in range(3)]
        q2 = qkv_ref[0, :, spots[0]]
        k2 = qkv_ref[0, :, spots[1]]
        v2 = qkv_ref[0, :, spots[2]]
        g2 = grad_ref[0, :, spots[0]]
        totals = [None, None, None]
        for half in range(2):
            mask = first if half == 0 else jnp.logical_not(first)

            def keep(v):
                return jnp.where(mask, v, jnp.zeros_like(v))

            probs = prob_ref[0, 2 * pair + half]
            g_half = keep(g2)
            grad_probs = dot_nt(v2, g_half)
            probs_wide = probs.astype(f32)
            delta = jnp.sum(grad_probs * probs_wide, axis=0, keepdims=True)
            grad_scores = (probs_wide * (grad_probs - delta)).astype(bf16)
            parts = (
                dot_tn(grad_scores, keep(k2)),
                dot_nn(grad_scores, keep(q2)),
                dot_nn(probs, g_half),
            )
            totals = [p if t is None else t + p for t, p in zip(totals, parts)]
        for part in range(3):
            value = totals[part] if part == 2 else totals[part] * scale
            value = value.astype(bf16)
            out_ref[0, :, spots[part]] = value
            sums_ref[:, spots[part]] += jnp.sum(value.astype(f32), axis=0, keepdims=True)


def attention(qkv, length):
    slots, rows, wide = qkv.shape
    width = wide // 3
    return pl.pallas_call(
        functools.partial(attention_kernel, length),
        grid=(slots,),
        in_specs=[pl.BlockSpec((1, rows, wide), lambda i: (i, 0, 0))],
        out_specs=[
            pl.BlockSpec((1, rows, width), lambda i: (i, 0, 0)),
            pl.BlockSpec((1, H, rows, rows), lambda i: (i, 0, 0, 0)),
        ],
        out_shape=[
            jax.ShapeDtypeStruct((slots, rows, width), bf16),
            pltpu.HBM((slots, H, rows, rows), bf16),
        ],
        compiler_params=pltpu.CompilerParams(vmem_limit_bytes=28 * 2**20),
        cost_estimate=FREE,
        name="attention",
    )(qkv)


def attention_back(qkv, probs, grad):
    slots, rows, wide = qkv.shape
    width = wide // 3
    return pl.pallas_call(
        attention_back_kernel,
        grid=(slots,),
        in_specs=[
            pl.BlockSpec((1, rows, wide), lambda i: (i, 0, 0)),
            pl.BlockSpec((1, H, rows, rows), lambda i: (i, 0, 0, 0)),
            pl.BlockSpec((1, rows, width), lambda i: (i, 0, 0)),
        ],
        out_specs=[
            pl.BlockSpec((1, rows, wide), lambda i: (i, 0, 0)),
            pl.BlockSpec((1, wide), lambda i: (0, 0)),
        ],
        out_shape=[
            jax.ShapeDtypeStruct((slots, rows, wide), bf16),
            jax.ShapeDtypeStruct((1, wide), f32),
        ],
        compiler_params=pltpu.CompilerParams(vmem_limit_bytes=28 * 2**20),
        cost_estimate=FREE,
        name="attention_back",
    )(qkv, probs, grad)


def hidden_back_kernel(grad_ref, weight_ref, slope_ref, out_ref, sums_ref):
    grad = dot_nt(grad_ref[...], weight_ref[...]) * slope_ref[...].astype(f32)
    grad = grad.astype(bf16)
    out_ref[...] = grad
    sums_ref[...] = jnp.sum(grad.astype(f32), axis=0, keepdims=True)


def hidden_back(grad, weight, slope):
    rows, width = grad.shape
    wide = weight.shape[0]
    tile = 512
    return pl.pallas_call(
        hidden_back_kernel,
        grid=(wide // tile,),
        in_specs=[
            pl.BlockSpec((rows, width), lambda i: (0, 0)),
            pl.BlockSpec((tile, width), lambda i: (i, 0)),
            pl.BlockSpec((rows, tile), lambda i: (0, i)),
        ],
        out_specs=[
            pl.BlockSpec((rows, tile), lambda i: (0, i)),
            pl.BlockSpec((1, tile), lambda i: (0, i)),
        ],
        out_shape=[
            jax.ShapeDtypeStruct((rows, wide), bf16),
            jax.ShapeDtypeStruct((1, wide), f32),
        ],
        compiler_params=pltpu.CompilerParams(vmem_limit_bytes=28 * 2**20),
        cost_estimate=FREE,
        name="hidden_back",
    )(grad, weight, slope)


def norm_back_kernel(grad_ref, weight_ref, value_ref, gain_ref, past_ref, out_ref, low_ref, sums_ref):
    upstream = dot_nt(grad_ref[...], weight_ref[...])
    normal, inverse = norm_parts(value_ref[...].astype(f32))

    @pl.when(pl.program_id(0) == 0)
    def _():
        sums_ref[...] = jnp.zeros_like(sums_ref)

    sums_ref[0:1] += jnp.sum(upstream * normal, axis=0, keepdims=True)
    sums_ref[1:2] += jnp.sum(upstream, axis=0, keepdims=True)
    total = past_ref[...].astype(f32) + norm_back(upstream * gain_ref[...], normal, inverse)
    low = total.astype(bf16)
    out_ref[...] = total
    low_ref[...] = low
    sums_ref[2:3] += jnp.sum(low.astype(f32), axis=0, keepdims=True)


def norm_back_low_kernel(grad_ref, weight_ref, value_ref, gain_ref, past_ref, low_ref, sums_ref):
    upstream = dot_nt(grad_ref[...], weight_ref[...])
    normal, inverse = norm_parts(value_ref[...].astype(f32))

    @pl.when(pl.program_id(0) == 0)
    def _():
        sums_ref[...] = jnp.zeros_like(sums_ref)

    sums_ref[0:1] += jnp.sum(upstream * normal, axis=0, keepdims=True)
    sums_ref[1:2] += jnp.sum(upstream, axis=0, keepdims=True)
    total = past_ref[...].astype(f32) + norm_back(upstream * gain_ref[...], normal, inverse)
    low_ref[...] = total.astype(bf16)


def matmul_norm_back(grad, weight, values, gain, past, count, both):
    rows, wide = grad.shape
    width = weight.shape[0]
    tile = rows // count
    tall = pl.BlockSpec((tile, width), lambda i: (i, 0))
    outs = [jax.ShapeDtypeStruct((rows, width), f32)] if both else []
    outs += [jax.ShapeDtypeStruct((rows, width), bf16), jax.ShapeDtypeStruct((8, width), f32)]
    return pl.pallas_call(
        norm_back_kernel if both else norm_back_low_kernel,
        grid=(count,),
        in_specs=[
            pl.BlockSpec((tile, wide), lambda i: (i, 0)),
            pl.BlockSpec((width, wide), lambda i: (0, 0)),
            tall,
            pl.BlockSpec((1, width), lambda i: (0, 0)),
            tall,
        ],
        out_specs=[tall] * (len(outs) - 1) + [pl.BlockSpec((8, width), lambda i: (0, 0))],
        out_shape=outs,
        compiler_params=pltpu.CompilerParams(vmem_limit_bytes=28 * 2**20),
        cost_estimate=FREE,
        name="matmul_norm_back",
    )(grad, weight, values, gain.reshape(1, width), past)


class Net:
    def __init__(self, rep_bits, shard_bits):
        self.core, self.x, self.y = rep_bits[-1], rep_bits[-2], rep_bits[-3]
        self.extra = tuple(rep_bits[:-3])
        self.rep = tuple(rep_bits)
        self.shard = tuple(shard_bits)
        self.bit = {name: lax.axis_index(name) for name in self.rep + self.shard}

    def other_way(self, name):
        return self.y if name == self.x else self.x

    def swap(self, piece, name):
        return lax.ppermute(piece, name, SWAP)

    def place(self, mine, other, name):
        bit = self.bit[name]
        return jnp.where(bit == 0, mine, other), jnp.where(bit == 0, other, mine)

    def join(self, piece, other, name, spot):
        return jnp.stack(self.place(piece, other, name), axis=spot)

    def grow(self, piece, name, spot):
        return self.join(piece, self.swap(piece, name), name, spot)

    def part_with(self, piece, name, spot):
        bit = self.bit[name]
        send = lax.dynamic_index_in_dim(piece, 1 - bit, spot, keepdims=False)
        keep = lax.dynamic_index_in_dim(piece, bit, spot, keepdims=False)
        return keep, self.swap(send, name)

    def core_half(self, matrix, other=False):
        half = matrix.shape[1] // 2
        bit = self.bit[self.core]
        return lax.dynamic_slice_in_dim(matrix, ((1 - bit) if other else bit) * half, half, 1)

    def both_cores(self, piece):
        return self.place(piece, self.swap(piece, self.core), self.core)

    def row_half(self, matrix, name):
        rows = matrix.shape[0] // 2
        return lax.dynamic_slice_in_dim(matrix, self.bit[name] * rows, rows, 0)

    def group_up(self, values):
        for spot, name in enumerate(self.shard):
            values = self.grow(values, name, spot)
        return values

    def place_in_group(self):
        me = 0
        for name in self.shard:
            me = 2 * me + self.bit[name]
        return me


def add(pair):
    return (pair[0].astype(f32) + pair[1].astype(f32)).astype(bf16)


def together(*values):
    return lax.optimization_barrier(values)


def cut_of(columns):
    return -(-columns // 256) * 128


def per_device(
    rep_bits,
    shard_bits,
    tokens,
    counts,
    w_qkv,
    b_query,
    b_value,
    w_proj,
    b_proj,
    gain_one,
    bias_one,
    gain_two,
    bias_two,
    w_up,
    b_up,
    w_down,
    b_down,
    out_grad,
):
    net = Net(rep_bits, shard_bits)
    group = 2 ** len(shard_bits)
    slot_count, length, width = tokens.shape
    padded = -(-length // 16) * 16
    row_count = slot_count * padded
    wide = w_up.shape[1]
    part = width // group
    blocks = w_down.shape[0] // part
    fill = ((0, 0), (0, padded - length), (0, 0))
    far, near = net.shard
    half_up, half_mid = wide // 2, width // 2

    plane = (net.x, net.y)

    def ways(piece):
        cut = cut_of(piece.shape[-1])
        return [piece[..., :cut], piece[..., cut:]]

    def fetch(mine):
        return jnp.concatenate(
            [net.row_half(p, name) for p, name in zip(ways(mine), plane)], axis=1
        )

    def send_plane(piece):
        return [net.swap(p, name) for p, name in zip(ways(piece), plane)]

    def join_plane(piece, others, spot):
        pairs = zip(ways(piece), others, plane)
        return jnp.concatenate(
            [net.join(p, o, name, spot).reshape(-1, p.shape[-1]) for p, o, name in pairs], axis=1
        )

    small = jnp.stack(
        [b_query, b_value, b_proj, gain_one, bias_one, gain_two, bias_two, b_down]
    )
    small = jnp.concatenate([small, b_up.reshape(-1, part)], axis=0)
    q_way = net.grow(fetch(net.core_half(w_qkv)), far, 0)
    small = net.grow(small, far, 0)
    mid_way = fetch(jnp.concatenate([net.core_half(w_up), net.core_half(w_proj)], axis=1))
    q_way, small, mid_way = together(q_way, small, mid_way)
    q_way = net.grow(q_way, near, 1)
    small = net.grow(small, near, 1)
    mid_got = net.swap(mid_way, far)
    down_mine = net.core_half(w_down).reshape(blocks, part, half_mid)
    down_mine = jnp.concatenate([down_mine[i] for i in range(blocks)], axis=1)
    q_way, small, mid_way, down_mine, tokens = together(
        q_way, small, mid_way, down_mine, tokens
    )
    q_got = send_plane(q_way)
    mid_way = net.join(mid_way, mid_got, far, 0)
    small = small.astype(f32).reshape(group, -1, part)
    rows = small[:, :8].transpose(1, 0, 2).reshape(8, width)
    query_bias, value_bias, proj_bias, gain_1, bias_1, gain_2, bias_2, down_bias = (
        rows[i] for i in range(8)
    )
    up_bias = small[:, 8:].reshape(wide)
    mid_way, down_way = together(mid_way, fetch(down_mine))
    mid_got = net.swap(mid_way, near)
    q_way, down_way = together(join_plane(q_way, q_got, 2), down_way)
    qkv_full = jnp.concatenate(net.both_cores(q_way), axis=1)

    live_slots = (jnp.arange(slot_count, dtype=jnp.int32) < counts[0]).astype(f32)
    live_rows = jnp.repeat(live_slots, padded)[:, None]
    low_inputs = jnp.pad(tokens, fill).reshape(row_count, width)
    inputs = low_inputs.astype(f32)
    normal_one, inverse_one = norm_parts(inputs)
    normed_one = (normal_one * gain_1 + bias_1).astype(bf16)
    qkv_bias = jnp.concatenate([query_bias, jnp.zeros_like(query_bias), value_bias])
    joined = (dot_nn(normed_one, qkv_full) + qkv_bias).astype(bf16)
    joined = joined.reshape(slot_count, padded, 3 * width)
    joined, mid_way = together(joined, mid_way)
    mid_way = net.join(mid_way, mid_got, near, 1)
    joined, mid_way, down_way = together(joined, mid_way, down_way)
    mid_got = send_plane(mid_way)
    down_got = net.swap(down_way, far)
    mixed, probs = attention(joined, length)
    mixed, mid_way, down_way, out_grad = together(mixed, mid_way, down_way, out_grad)
    mid_way = join_plane(mid_way, mid_got, 2)
    down_way = net.join(down_way, down_got, far, 0)
    mixed, mid_way, down_way = together(mixed, mid_way, down_way)
    down_got = net.swap(down_way, near)
    *mid_pairs, down_way = together(*net.both_cores(mid_way), down_way)
    down_way = net.join(down_way, down_got, near, 1)
    down_got = send_plane(down_way)
    mixed = mixed.reshape(row_count, width)
    mid = mid_pairs
    up_full = jnp.concatenate([m[:, :half_up] for m in mid], axis=1)
    proj_full = jnp.concatenate([m[:, half_up:] for m in mid], axis=1)
    middle = inputs + (dot_nn(mixed, proj_full) + proj_bias)
    normal_two, inverse_two = norm_parts(middle)
    normed_two = (normal_two * gain_2 + bias_2).astype(bf16)
    hidden = dot_nn(normed_two, up_full) + up_bias
    share = 0.5 * (1.0 + lax.erf(hidden * ROOT_HALF))
    active = (hidden * share).astype(bf16)
    active, down_way = together(active, down_way)
    down_pairs = net.both_cores(join_plane(down_way, down_got, 2))
    slope = (share + hidden * jnp.exp(-0.5 * hidden * hidden) * INV_ROOT_TAU).astype(bf16)
    down = [
        jnp.stack(
            [
                d.reshape(group, part, -1)[:, :, b * half_mid : (b + 1) * half_mid]
                for b in range(blocks)
            ],
            axis=1,
        )
        for d in down_pairs
    ]
    down_full = jnp.concatenate(down, axis=3).reshape(wide, width)

    def start_sum(left, right):
        return dot_tn(left, net.core_half(right, True)).astype(bf16)

    def own_sum(left, right, other):
        total = dot_tn(left, net.core_half(right)) + other.astype(f32)
        total = total.astype(bf16)
        return total.reshape(2, 2, 2, -1, total.shape[1])

    def part_plane(piece):
        pairs = [net.part_with(p, name, 2) for p, name in zip(ways(piece), plane)]
        return [p[0] for p in pairs], [p[1] for p in pairs]

    def add_plane(keeps, others):
        return jnp.concatenate([add(pair) for pair in zip(keeps, others)], axis=-1)

    def exchange_plane(piece):
        done = []
        for p, name in zip(ways(piece), plane):
            for other in (net.other_way(name),) + net.extra:
                p = add((p, net.swap(p, other)))
            done.append(p)
        return done

    def grow_plane(pieces):
        return jnp.concatenate(
            [
                net.grow(p, name, 0).reshape(-1, p.shape[-1])
                for p, name in zip(pieces, plane)
            ],
            axis=1,
        )

    grad_branch = jnp.pad(out_grad, fill).reshape(row_count, width)
    grad_branch = grad_branch * live_rows.astype(bf16)
    grad_down_b = jnp.sum(grad_branch.astype(f32), axis=0, keepdims=True)
    branch_2, d_send = together(grad_branch, start_sum(active, grad_branch))
    d_other = net.swap(d_send, net.core)
    result = middle + (dot_nn(active, down_full) + down_bias)
    layer_out = (result * live_rows).astype(bf16)
    layer_out = layer_out.reshape(slot_count, padded, width)[:, :length]
    branch_3, layer_out = together(grad_branch, layer_out)
    d_piece = own_sum(active, branch_3, d_other)
    branch_2, d_piece = together(branch_2, d_piece)
    d_keeps, d_others = part_plane(d_piece)
    grad_hidden, up_sums = hidden_back(branch_2, down_full, slope)
    grad_hidden, u_send = together(grad_hidden, start_sum(normed_two, grad_hidden))
    u_other = net.swap(u_send, net.core)
    grad_middle, grad_attn, mid_sums = matmul_norm_back(
        grad_hidden, up_full, middle, gain_2, grad_branch, slot_count, True
    )
    grad_attn, *d_keeps = together(grad_attn, *d_keeps)
    d_piece = add_plane(d_keeps, d_others)
    grad_hidden, grad_attn, d_piece = together(grad_hidden, grad_attn, d_piece)
    d_pair = net.part_with(d_piece, near, 1)
    grad_attn, p_send = together(grad_attn, start_sum(mixed, grad_attn))
    p_other = net.swap(p_send, net.core)
    u_piece = own_sum(normed_two, grad_hidden, u_other)
    grad_attn, u_piece = together(grad_attn, u_piece)
    p_piece = own_sum(mixed, grad_attn, p_other)
    grad_attn_2, u_piece = together(grad_attn, jnp.concatenate([u_piece, p_piece], axis=-1))
    u_keeps, u_others = part_plane(u_piece)
    grad_mixed = dot_nt(grad_attn_2, proj_full).astype(bf16)
    grad_joined, joined_sums = attention_back(
        joined, probs, grad_mixed.reshape(slot_count, padded, width)
    )
    grad_joined, d_keep, *u_keeps = together(
        grad_joined.reshape(row_count, 3 * width), d_pair[0], *u_keeps
    )
    d_piece = add((d_keep, d_pair[1]))
    u_piece = add_plane(u_keeps, u_others)
    grad_joined, d_piece, u_piece = together(grad_joined, d_piece, u_piece)
    d_pair = net.part_with(d_piece, far, 0)
    u_pair = net.part_with(u_piece, near, 1)
    grad_joined, q_send = together(grad_joined, start_sum(normed_one, grad_joined))
    q_other = net.swap(q_send, net.core)
    q_piece = own_sum(normed_one, grad_joined, q_other)
    grad_joined, q_piece = together(grad_joined, q_piece)
    q_keeps, q_others = part_plane(q_piece)
    grad_tokens, first_sums = matmul_norm_back(
        grad_joined, qkv_full, low_inputs, gain_1, grad_middle, slot_count, False
    )
    grad_tokens = grad_tokens.reshape(slot_count, padded, width)[:, :length]

    vectors = [
        mid_sums[2:3],
        mid_sums[0:2],
        grad_down_b,
        joined_sums[:, :width],
        joined_sums[:, 2 * width :],
        first_sums[0:2],
    ]
    vectors += [up_sums[:, k * width : (k + 1) * width] for k in range(group)]
    vectors = jnp.concatenate(vectors, axis=0)

    vectors, u_keep, *q_keeps = together(vectors, u_pair[0], *q_keeps)
    sums = vectors + net.swap(vectors, net.core)
    q_piece = add_plane(q_keeps, q_others)
    q_piece, u_keep, d_keep, sums = together(q_piece, u_keep, d_pair[0], sums)
    q_pair = net.part_with(q_piece, near, 1)
    u_piece = add((u_keep, u_pair[1]))
    u_piece, d_keep, sums, q_keep = together(u_piece, d_keep, sums, q_pair[0])
    u_pair = net.part_with(u_piece, far, 0)
    d_piece = exchange_plane(add((d_keep, d_pair[1])))
    sums = sums + net.swap(sums, net.x)
    q_piece = add((q_keep, q_pair[1]))
    q_piece, u_keep, sums, *d_piece = together(q_piece, u_pair[0], sums, *d_piece)
    q_pair = net.part_with(q_piece, far, 0)
    down_shard = grow_plane(d_piece)
    sums = sums + net.swap(sums, net.y)
    u_piece = exchange_plane(add((u_keep, u_pair[1])))
    q_keep, sums, down_shard, *u_piece = together(q_pair[0], sums, down_shard, *u_piece)
    q_piece = add((q_keep, q_pair[1]))
    up_shard = grow_plane(u_piece)
    down_pair = net.both_cores(down_shard)
    sums = sums + net.swap(sums, far)
    q_1, q_2 = exchange_plane(q_piece)
    q_1, q_2, sums, up_shard = together(q_1, q_2, sums, up_shard)
    up_pair = net.both_cores(up_shard)
    q_pair = net.both_cores(grow_plane([q_1, q_2]))
    for name in (near,) + net.extra:
        sums = sums + net.swap(sums, name)
    me = net.place_in_group()
    owned = lax.dynamic_slice_in_dim(sums[:8], me * part, part, 1)
    owned_up = lax.dynamic_index_in_dim(sums, 8 + me, 0, keepdims=False)
    grad_down_w = jnp.concatenate(down_pair, axis=1).astype(f32)
    grad_up_w = jnp.concatenate([p[:, :half_up] for p in up_pair], axis=1).astype(f32)
    grad_proj_w = jnp.concatenate([p[:, half_up:] for p in up_pair], axis=1).astype(f32)
    grad_qkv_w = jnp.concatenate(q_pair, axis=1).astype(f32)
    return (
        layer_out,
        grad_tokens,
        grad_qkv_w,
        owned[4],
        owned[5],
        grad_proj_w,
        owned[0],
        owned[6],
        owned[7],
        owned[1],
        owned[2],
        grad_up_w,
        owned_up,
        grad_down_w,
        owned[3],
    )


def solution(mesh):
    rep, shard = mesh.shape["rep"], mesh.shape["shard"]
    rep_bits = tuple(f"r{i}" for i in range(rep.bit_length() - 1))
    shard_bits = tuple(f"s{i}" for i in range(shard.bit_length() - 1))
    fine = Mesh(mesh.devices.reshape((2,) * (len(rep_bits) + len(shard_bits))), rep_bits + shard_bits)
    every = P(rep_bits + shard_bits, None, None)
    matrix = P(shard_bits, None)
    vector = P(shard_bits)
    return jax.shard_map(
        functools.partial(per_device, rep_bits, shard_bits),
        mesh=fine,
        in_specs=(
            every,
            P(rep_bits + shard_bits),
            matrix,
            vector,
            vector,
            matrix,
            vector,
            vector,
            vector,
            vector,
            vector,
            matrix,
            vector,
            matrix,
            vector,
            every,
        ),
        out_specs=(
            every,
            every,
            matrix,
            vector,
            vector,
            matrix,
            vector,
            vector,
            vector,
            vector,
            vector,
            matrix,
            vector,
            matrix,
            vector,
        ),
        check_vma=False,
    )
```

```python
import functools
import math

import jax
import jax.numpy as jnp
from jax import lax
from jax.experimental import pallas as pl
from jax.experimental.pallas import tpu as pltpu
from jax.sharding import Mesh, PartitionSpec as P

H = 12
HD = 64
EPSILON = 1e-06
ROOT_HALF = 1.0 / math.sqrt(2.0)
INV_ROOT_TAU = 1.0 / math.sqrt(2.0 * math.pi)
f32 = jnp.float32
bf16 = jnp.bfloat16
SWAP = [(0, 1), (1, 0)]
FREE = pl.CostEstimate(flops=0, bytes_accessed=0, transcendentals=0)


def norm_parts(values_in):
    row_mean = jnp.mean(values_in, axis=-1, keepdims=True)
    centred = values_in - row_mean
    inverse = lax.rsqrt(jnp.mean(centred * centred, axis=-1, keepdims=True) + EPSILON)
    return (centred * inverse, inverse)


def norm_back(grad_normal, normal_rows, inverse_rows):
    first_mean = jnp.mean(grad_normal, axis=-1, keepdims=True)
    second_mean = jnp.mean(grad_normal * normal_rows, axis=-1, keepdims=True)
    return inverse_rows * (grad_normal - first_mean - normal_rows * second_mean)


def dot_nt(a, b):
    return lax.dot_general(a, b, (((1,), (1,)), ((), ())), preferred_element_type=f32)


def dot_tn(a, b):
    return lax.dot_general(a, b, (((0,), (0,)), ((), ())), preferred_element_type=f32)


def dot_nn(a, b):
    return jnp.dot(a, b, preferred_element_type=f32)


def attention_kernel(length, qkv_ref, out_ref, prob_ref):
    rows = qkv_ref.shape[1]
    width = H * HD
    first = lax.broadcasted_iota(jnp.int32, (1, 2 * HD), 1) < HD
    key_live = lax.broadcasted_iota(jnp.int32, (rows, 1), 0) < length
    for pair in range(H // 2):
        lanes = pl.ds(pair * 2 * HD, 2 * HD)
        q2 = qkv_ref[0, :, pl.ds(pair * 2 * HD, 2 * HD)] * jnp.asarray(HD ** (-0.5), bf16)
        k2 = qkv_ref[0, :, pl.ds(width + pair * 2 * HD, 2 * HD)]
        v2 = qkv_ref[0, :, pl.ds(2 * width + pair * 2 * HD, 2 * HD)]
        total = None
        for half in range(2):
            mask = first if half == 0 else jnp.logical_not(first)
            scores = dot_nt(jnp.where(mask, k2, jnp.zeros_like(k2)), q2)
            scores = jnp.where(key_live, scores, -1e30)
            expo = jnp.exp(scores - jnp.max(scores, axis=0, keepdims=True))
            probs = (expo * (1.0 / jnp.sum(expo, axis=0, keepdims=True))).astype(bf16)
            prob_ref[0, 2 * pair + half] = probs
            part = dot_tn(probs, jnp.where(mask, v2, jnp.zeros_like(v2)))
            total = part if total is None else total + part
        out_ref[0, :, lanes] = total.astype(bf16)


def attention_back_kernel(qkv_ref, prob_ref, grad_ref, out_ref, sums_ref):
    width = H * HD
    first = lax.broadcasted_iota(jnp.int32, (1, 2 * HD), 1) < HD
    scale = jnp.asarray(HD ** (-0.5), f32)

    @pl.when(pl.program_id(0) == 0)
    def _():
        sums_ref[...] = jnp.zeros_like(sums_ref)

    for pair in range(H // 2):
        spots = [pl.ds(part * width + pair * 2 * HD, 2 * HD) for part in range(3)]
        q2 = qkv_ref[0, :, spots[0]]
        k2 = qkv_ref[0, :, spots[1]]
        v2 = qkv_ref[0, :, spots[2]]
        g2 = grad_ref[0, :, spots[0]]
        totals = [None, None, None]
        for half in range(2):
            mask = first if half == 0 else jnp.logical_not(first)

            def keep(v):
                return jnp.where(mask, v, jnp.zeros_like(v))

            probs = prob_ref[0, 2 * pair + half]
            g_half = keep(g2)
            grad_probs = dot_nt(v2, g_half)
            probs_wide = probs.astype(f32)
            delta = jnp.sum(grad_probs * probs_wide, axis=0, keepdims=True)
            grad_scores = (probs_wide * (grad_probs - delta)).astype(bf16)
            parts = (
                dot_tn(grad_scores, keep(k2)),
                dot_nn(grad_scores, keep(q2)),
                dot_nn(probs, g_half),
            )
            totals = [p if t is None else t + p for t, p in zip(totals, parts)]
        for part in range(3):
            value = totals[part] if part == 2 else totals[part] * scale
            value = value.astype(bf16)
            out_ref[0, :, spots[part]] = value
            sums_ref[:, spots[part]] += jnp.sum(value.astype(f32), axis=0, keepdims=True)


def stay(value):
    return pltpu.with_memory_space_constraint(value, pltpu.HBM)


def attention(qkv, length):
    slots, rows, wide = qkv.shape
    width = wide // 3
    return pl.pallas_call(
        functools.partial(attention_kernel, length),
        grid=(slots,),
        in_specs=[pl.BlockSpec((1, rows, wide), lambda i: (i, 0, 0))],
        out_specs=[
            pl.BlockSpec((1, rows, width), lambda i: (i, 0, 0)),
            pl.BlockSpec((1, H, rows, rows), lambda i: (i, 0, 0, 0)),
        ],
        out_shape=[
            jax.ShapeDtypeStruct((slots, rows, width), bf16),
            pltpu.HBM((slots, H, rows, rows), bf16),
        ],
        compiler_params=pltpu.CompilerParams(vmem_limit_bytes=28 * 2**20),
        cost_estimate=FREE,
        name="attention",
    )(qkv)


def attention_back(qkv, probs, grad):
    slots, rows, wide = qkv.shape
    width = wide // 3
    return pl.pallas_call(
        attention_back_kernel,
        grid=(slots,),
        in_specs=[
            pl.BlockSpec((1, rows, wide), lambda i: (i, 0, 0)),
            pl.BlockSpec((1, H, rows, rows), lambda i: (i, 0, 0, 0)),
            pl.BlockSpec((1, rows, width), lambda i: (i, 0, 0)),
        ],
        out_specs=[
            pl.BlockSpec((1, rows, wide), lambda i: (i, 0, 0)),
            pl.BlockSpec((1, wide), lambda i: (0, 0)),
        ],
        out_shape=[
            jax.ShapeDtypeStruct((slots, rows, wide), bf16),
            jax.ShapeDtypeStruct((1, wide), f32),
        ],
        compiler_params=pltpu.CompilerParams(vmem_limit_bytes=28 * 2**20),
        cost_estimate=FREE,
        name="attention_back",
    )(qkv, stay(probs), grad)


def hidden_back_kernel(grad_ref, weight_ref, slope_ref, out_ref, sums_ref):
    grad = dot_nt(grad_ref[...], weight_ref[...]) * slope_ref[...].astype(f32)
    grad = grad.astype(bf16)
    out_ref[...] = grad
    sums_ref[...] = jnp.sum(grad.astype(f32), axis=0, keepdims=True)


def hidden_back(grad, weight, slope):
    rows, width = grad.shape
    wide = weight.shape[0]
    tile = 512
    return pl.pallas_call(
        hidden_back_kernel,
        grid=(wide // tile,),
        in_specs=[
            pl.BlockSpec((rows, width), lambda i: (0, 0)),
            pl.BlockSpec((tile, width), lambda i: (i, 0)),
            pl.BlockSpec((rows, tile), lambda i: (0, i)),
        ],
        out_specs=[
            pl.BlockSpec((rows, tile), lambda i: (0, i)),
            pl.BlockSpec((1, tile), lambda i: (0, i)),
        ],
        out_shape=[
            pltpu.HBM((rows, wide), bf16),
            jax.ShapeDtypeStruct((1, wide), f32),
        ],
        compiler_params=pltpu.CompilerParams(vmem_limit_bytes=28 * 2**20),
        cost_estimate=FREE,
        name="hidden_back",
    )(grad, weight, slope)


def norm_back_kernel(grad_ref, weight_ref, value_ref, gain_ref, past_ref, out_ref, low_ref, sums_ref):
    upstream = dot_nt(grad_ref[...], weight_ref[...])
    normal, inverse = norm_parts(value_ref[...].astype(f32))

    @pl.when(pl.program_id(0) == 0)
    def _():
        sums_ref[...] = jnp.zeros_like(sums_ref)

    sums_ref[0:1] += jnp.sum(upstream * normal, axis=0, keepdims=True)
    sums_ref[1:2] += jnp.sum(upstream, axis=0, keepdims=True)
    total = past_ref[...].astype(f32) + norm_back(upstream * gain_ref[...], normal, inverse)
    low = total.astype(bf16)
    out_ref[...] = total
    low_ref[...] = low
    sums_ref[2:3] += jnp.sum(low.astype(f32), axis=0, keepdims=True)


def norm_back_low_kernel(grad_ref, weight_ref, value_ref, gain_ref, past_ref, low_ref, sums_ref):
    upstream = dot_nt(grad_ref[...], weight_ref[...])
    normal, inverse = norm_parts(value_ref[...].astype(f32))

    @pl.when(pl.program_id(0) == 0)
    def _():
        sums_ref[...] = jnp.zeros_like(sums_ref)

    sums_ref[0:1] += jnp.sum(upstream * normal, axis=0, keepdims=True)
    sums_ref[1:2] += jnp.sum(upstream, axis=0, keepdims=True)
    total = past_ref[...].astype(f32) + norm_back(upstream * gain_ref[...], normal, inverse)
    low_ref[...] = total.astype(bf16)


def matmul_norm_back(grad, weight, values, gain, past, count, both):
    rows, wide = grad.shape
    width = weight.shape[0]
    tile = rows // count
    tall = pl.BlockSpec((tile, width), lambda i: (i, 0))
    outs = [jax.ShapeDtypeStruct((rows, width), f32)] if both else []
    outs += [jax.ShapeDtypeStruct((rows, width), bf16), jax.ShapeDtypeStruct((8, width), f32)]
    return pl.pallas_call(
        norm_back_kernel if both else norm_back_low_kernel,
        grid=(count,),
        in_specs=[
            pl.BlockSpec((tile, wide), lambda i: (i, 0)),
            pl.BlockSpec((width, wide), lambda i: (0, 0)),
            tall,
            pl.BlockSpec((1, width), lambda i: (0, 0)),
            tall,
        ],
        out_specs=[tall] * (len(outs) - 1) + [pl.BlockSpec((8, width), lambda i: (0, 0))],
        out_shape=outs,
        compiler_params=pltpu.CompilerParams(vmem_limit_bytes=28 * 2**20),
        cost_estimate=FREE,
        name="matmul_norm_back",
    )(*map(stay if both else (lambda v: v), (grad, weight, values)), gain.reshape(1, width), past)


class Net:
    def __init__(self, rep_bits, shard_bits):
        self.core, self.x, self.y = rep_bits[-1], rep_bits[-2], rep_bits[-3]
        self.extra = tuple(rep_bits[:-3])
        self.rep = tuple(rep_bits)
        self.shard = tuple(shard_bits)
        self.bit = {name: lax.axis_index(name) for name in self.rep + self.shard}

    def other_way(self, name):
        return self.y if name == self.x else self.x

    def swap(self, piece, name):
        return lax.ppermute(piece, name, SWAP)

    def place(self, mine, other, name):
        bit = self.bit[name]
        return jnp.where(bit == 0, mine, other), jnp.where(bit == 0, other, mine)

    def join(self, piece, other, name, spot):
        return jnp.stack(self.place(piece, other, name), axis=spot)

    def grow(self, piece, name, spot):
        return self.join(piece, self.swap(piece, name), name, spot)

    def part_with(self, piece, name, spot):
        bit = self.bit[name]
        send = lax.dynamic_index_in_dim(piece, 1 - bit, spot, keepdims=False)
        keep = lax.dynamic_index_in_dim(piece, bit, spot, keepdims=False)
        return keep, self.swap(send, name)

    def core_half(self, matrix, other=False):
        half = matrix.shape[1] // 2
        bit = self.bit[self.core]
        return lax.dynamic_slice_in_dim(matrix, ((1 - bit) if other else bit) * half, half, 1)

    def both_cores(self, piece):
        return self.place(piece, self.swap(piece, self.core), self.core)

    def row_half(self, matrix, name):
        rows = matrix.shape[0] // 2
        return lax.dynamic_slice_in_dim(matrix, self.bit[name] * rows, rows, 0)

    def group_up(self, values):
        for spot, name in enumerate(self.shard):
            values = self.grow(values, name, spot)
        return values

    def place_in_group(self):
        me = 0
        for name in self.shard:
            me = 2 * me + self.bit[name]
        return me


def add(pair):
    return (pair[0].astype(f32) + pair[1].astype(f32)).astype(bf16)


def together(*values):
    return lax.optimization_barrier(values)


def cut_of(columns):
    return -(-columns // 256) * 128


def per_device(
    rep_bits,
    shard_bits,
    tokens,
    counts,
    w_qkv,
    b_query,
    b_value,
    w_proj,
    b_proj,
    gain_one,
    bias_one,
    gain_two,
    bias_two,
    w_up,
    b_up,
    w_down,
    b_down,
    out_grad,
):
    net = Net(rep_bits, shard_bits)
    group = 2 ** len(shard_bits)
    slot_count, length, width = tokens.shape
    padded = -(-length // 16) * 16
    row_count = slot_count * padded
    wide = w_up.shape[1]
    part = width // group
    blocks = w_down.shape[0] // part
    fill = ((0, 0), (0, padded - length), (0, 0))
    far, near = net.shard
    half_up, half_mid = wide // 2, width // 2

    plane = (net.x, net.y)

    def ways(piece):
        cut = cut_of(piece.shape[-1])
        return [piece[..., :cut], piece[..., cut:]]

    def fetch(mine):
        return jnp.concatenate(
            [net.row_half(p, name) for p, name in zip(ways(mine), plane)], axis=1
        )

    def send_plane(piece):
        return [net.swap(p, name) for p, name in zip(ways(piece), plane)]

    def join_plane(piece, others, spot):
        pairs = zip(ways(piece), others, plane)
        return jnp.concatenate(
            [net.join(p, o, name, spot).reshape(-1, p.shape[-1]) for p, o, name in pairs], axis=1
        )

    small = jnp.stack(
        [b_query, b_value, b_proj, gain_one, bias_one, gain_two, bias_two, b_down]
    )
    small = jnp.concatenate([small, b_up.reshape(-1, part)], axis=0)
    q_way = net.grow(fetch(net.core_half(w_qkv)), far, 0)
    small = net.grow(small, far, 0)
    mid_way = fetch(jnp.concatenate([net.core_half(w_up), net.core_half(w_proj)], axis=1))
    q_way, small = together(q_way, small)
    q_way = net.grow(q_way, near, 1)
    small = net.grow(small, near, 1)
    down_mine = net.core_half(w_down).reshape(blocks, part, half_mid)
    down_mine = jnp.concatenate([down_mine[i] for i in range(blocks)], axis=1)
    q_way, small, mid_way, down_mine, tokens = together(
        q_way, small, mid_way, down_mine, tokens
    )
    q_got = send_plane(q_way)
    mid_got = net.swap(mid_way, far)
    small = small.astype(f32).reshape(group, -1, part)
    rows = small[:, :8].transpose(1, 0, 2).reshape(8, width)
    query_bias, value_bias, proj_bias, gain_1, bias_1, gain_2, bias_2, down_bias = (
        rows[i] for i in range(8)
    )
    up_bias = small[:, 8:].reshape(wide)
    q_way, *q_got = together(q_way, *q_got)
    q_way, mid_way, down_way = together(join_plane(q_way, q_got, 2), mid_way, fetch(down_mine))
    qkv_pair = net.both_cores(q_way)
    mid_way = net.join(mid_way, mid_got, far, 0)
    mid_got = net.swap(mid_way, near)
    (qkv_full,) = together(jnp.concatenate(qkv_pair, axis=1))

    live_slots = (jnp.arange(slot_count, dtype=jnp.int32) < counts[0]).astype(f32)
    live_rows = jnp.repeat(live_slots, padded)[:, None]
    low_inputs = jnp.pad(tokens, fill).reshape(row_count, width)
    inputs = low_inputs.astype(f32)
    normal_one, inverse_one = norm_parts(inputs)
    normed_one = (normal_one * gain_1 + bias_1).astype(bf16)
    qkv_bias = jnp.concatenate([query_bias, jnp.zeros_like(query_bias), value_bias])
    joined = (dot_nn(normed_one, qkv_full) + qkv_bias).astype(bf16)
    joined = joined.reshape(slot_count, padded, 3 * width)
    mixed, probs = attention(joined, length)
    mixed, mid_way, mid_got, down_way = together(mixed, mid_way, mid_got, down_way)
    mid_way = net.join(mid_way, mid_got, near, 1)
    mixed, mid_way, down_way = together(mixed, mid_way, down_way)
    mid_got = send_plane(mid_way)
    down_got = net.swap(down_way, far)
    mixed, mid_way, down_way, out_grad, down_got, *mid_got = together(
        mixed, mid_way, down_way, out_grad, down_got, *mid_got
    )
    down_way = net.join(down_way, down_got, far, 0)
    mid_way, down_way = together(join_plane(mid_way, mid_got, 2), down_way)
    down_got = net.swap(down_way, near)
    *mid_pairs, down_way = together(*net.both_cores(mid_way), down_way)
    down_way = net.join(down_way, down_got, near, 1)
    down_got = send_plane(down_way)
    mixed = mixed.reshape(row_count, width)
    mid = mid_pairs
    up_full = jnp.concatenate([m[:, :half_up] for m in mid], axis=1)
    proj_full = jnp.concatenate([m[:, half_up:] for m in mid], axis=1)
    up_full, proj_full = together(up_full, proj_full)
    middle = inputs + (dot_nn(mixed, proj_full) + proj_bias)
    normal_two, inverse_two = norm_parts(middle)
    normed_two = (normal_two * gain_2 + bias_2).astype(bf16)
    hidden = dot_nn(normed_two, up_full) + up_bias
    share = 0.5 * (1.0 + lax.erf(hidden * ROOT_HALF))
    active = (hidden * share).astype(bf16)
    active, down_way = together(active, down_way)
    down_pairs = net.both_cores(join_plane(down_way, down_got, 2))
    slope = (share + hidden * jnp.exp(-0.5 * hidden * hidden) * INV_ROOT_TAU).astype(bf16)
    down = [
        jnp.stack(
            [
                d.reshape(group, part, -1)[:, :, b * half_mid : (b + 1) * half_mid]
                for b in range(blocks)
            ],
            axis=1,
        )
        for d in down_pairs
    ]
    (down_full,) = together(jnp.concatenate(down, axis=3).reshape(wide, width))

    def start_sum(left, right):
        return dot_tn(left, net.core_half(right, True)).astype(bf16)

    def own_sum(left, right, other):
        total = dot_tn(left, net.core_half(right)) + other.astype(f32)
        total = total.astype(bf16)
        return total.reshape(2, 2, 2, -1, total.shape[1])

    def part_plane(piece):
        pairs = [net.part_with(p, name, 2) for p, name in zip(ways(piece), plane)]
        return [p[0] for p in pairs], [p[1] for p in pairs]

    def add_plane(keeps, others):
        return jnp.concatenate([add(pair) for pair in zip(keeps, others)], axis=-1)

    def exchange_plane(piece):
        done = []
        for p, name in zip(ways(piece), plane):
            for other in (net.other_way(name),) + net.extra:
                p = add((p, net.swap(p, other)))
            done.append(p)
        return done

    def grow_plane(pieces):
        return jnp.concatenate(
            [
                net.grow(p, name, 0).reshape(-1, p.shape[-1])
                for p, name in zip(pieces, plane)
            ],
            axis=1,
        )

    grad_branch = jnp.pad(out_grad, fill).reshape(row_count, width)
    grad_branch = grad_branch * live_rows.astype(bf16)
    grad_down_b = jnp.sum(grad_branch.astype(f32), axis=0, keepdims=True)
    branch_2, d_send = together(grad_branch, start_sum(active, grad_branch))
    d_other = net.swap(d_send, net.core)
    result = middle + (dot_nn(active, down_full) + down_bias)
    layer_out = (result * live_rows).astype(bf16)
    layer_out = layer_out.reshape(slot_count, padded, width)[:, :length]
    branch_3, layer_out = together(grad_branch, layer_out)
    d_piece = own_sum(active, branch_3, d_other)
    branch_2, d_piece = together(branch_2, d_piece)
    fine = d_piece.shape[3] // 2
    d_pairs = [
        net.part_with(d_piece[:, :, :, i * fine : (i + 1) * fine], name, 2)
        for i, name in enumerate(plane)
    ]
    d_keeps, d_others = [p[0] for p in d_pairs], [p[1] for p in d_pairs]
    grad_hidden, up_sums = hidden_back(branch_2, down_full, slope)
    grad_hidden, u_send = together(grad_hidden, start_sum(normed_two, grad_hidden))
    u_other = net.swap(u_send, net.core)
    grad_middle, grad_attn, mid_sums = matmul_norm_back(
        grad_hidden, up_full, middle, gain_2, grad_branch, slot_count, True
    )
    grad_attn, d_1, d_2, o_1, o_2 = together(grad_attn, *d_keeps, *d_others)
    grad_hidden, grad_attn = together(grad_hidden, grad_attn)
    grad_attn, p_send = together(grad_attn, start_sum(mixed, grad_attn))
    p_other = net.swap(p_send, net.core)
    u_piece = own_sum(normed_two, grad_hidden, u_other)
    grad_attn, u_piece = together(grad_attn, u_piece)
    p_piece = own_sum(mixed, grad_attn, p_other)
    u_piece = jnp.concatenate([u_piece, p_piece], axis=-1)
    grad_attn_2, u_piece, d_1, d_2, o_1, o_2 = together(grad_attn, u_piece, d_1, d_2, o_1, o_2)
    d_piece = add_plane([d_1, d_2], [o_1, o_2])
    d_pair = net.part_with(d_piece, near, 1)
    u_keeps, u_others = part_plane(u_piece)
    grad_mixed = dot_nt(grad_attn_2, proj_full).astype(bf16)
    grad_joined, joined_sums = attention_back(
        joined, probs, grad_mixed.reshape(slot_count, padded, width)
    )
    grad_joined, d_keep, d_other, u_1, u_2, o_1, o_2 = together(
        grad_joined.reshape(row_count, 3 * width), *d_pair, *u_keeps, *u_others
    )
    grad_joined, q_send, d_keep, d_other, u_1, u_2, o_1, o_2 = together(
        grad_joined, start_sum(normed_one, grad_joined), d_keep, d_other, u_1, u_2, o_1, o_2
    )
    q_other = net.swap(q_send, net.core)
    u_piece = add_plane([u_1, u_2], [o_1, o_2])
    d_piece = add((d_keep, d_other))
    grad_joined, d_piece, u_piece = together(grad_joined, d_piece, u_piece)
    u_pair = net.part_with(u_piece, near, 1)
    d_pair = net.part_with(d_piece, far, 0)
    q_piece = own_sum(normed_one, grad_joined, q_other)
    grad_joined, q_piece = together(grad_joined, q_piece)
    q_keeps, q_others = part_plane(q_piece)
    grad_tokens, first_sums = matmul_norm_back(
        grad_joined, qkv_full, low_inputs, gain_1, grad_middle, slot_count, False
    )
    grad_tokens = grad_tokens.reshape(slot_count, padded, width)[:, :length]

    vectors = [
        mid_sums[2:3],
        mid_sums[0:2],
        grad_down_b,
        joined_sums[:, :width],
        joined_sums[:, 2 * width :],
        first_sums[0:2],
    ]
    vectors += [up_sums[:, k * width : (k + 1) * width] for k in range(group)]
    vectors = jnp.concatenate(vectors, axis=0)

    vectors, u_keep, u_other, d_keep, d_other, q_1, q_2, o_1, o_2 = together(
        vectors, *u_pair, *d_pair, *q_keeps, *q_others
    )
    q_piece = add_plane([q_1, q_2], [o_1, o_2])
    u_piece = add((u_keep, u_other))
    q_piece, u_piece, vectors, d_keep = together(q_piece, u_piece, vectors, d_keep)
    q_pair = net.part_with(q_piece, near, 1)
    u_pair = net.part_with(u_piece, far, 0)
    sums = vectors + net.swap(vectors, net.core)
    d_piece = exchange_plane(add((d_keep, d_other)))
    q_keep, q_other, u_keep, u_other, sums, *d_piece = together(*q_pair, *u_pair, sums, *d_piece)
    q_piece = add((q_keep, q_other))
    u_piece = add((u_keep, u_other))
    q_piece, u_piece, sums, *d_piece = together(q_piece, u_piece, sums, *d_piece)
    q_pair = net.part_with(q_piece, far, 0)
    u_piece = exchange_plane(u_piece)
    down_shard = jnp.stack(
        [net.grow(p, name, 0) for p, name in zip(d_piece, plane)], axis=1
    ).reshape(-1, half_mid)
    sums = sums + net.swap(sums, net.x)
    q_keep, q_other, sums, down_shard, *u_piece = together(*q_pair, sums, down_shard, *u_piece)
    q_1, q_2 = exchange_plane(add((q_keep, q_other)))
    up_shard = grow_plane(u_piece)
    down_pair = net.both_cores(down_shard)
    sums = sums + net.swap(sums, net.y)
    grad_down_w = jnp.concatenate(down_pair, axis=1).astype(f32)
    q_1, q_2, sums, up_shard, grad_down_w = together(q_1, q_2, sums, up_shard, grad_down_w)
    q_piece = grow_plane([q_1, q_2])
    up_pair = net.both_cores(up_shard)
    sums = sums + net.swap(sums, far)
    q_piece, sums, *up_pair = together(q_piece, sums, *up_pair)
    q_pair = net.both_cores(q_piece)
    for name in (near,) + net.extra:
        sums = sums + net.swap(sums, name)
    me = net.place_in_group()
    owned = lax.dynamic_slice_in_dim(sums[:8], me * part, part, 1)
    owned_up = lax.dynamic_index_in_dim(sums, 8 + me, 0, keepdims=False)
    grad_up_w = jnp.concatenate([p[:, :half_up] for p in up_pair], axis=1).astype(f32)
    grad_proj_w = jnp.concatenate([p[:, half_up:] for p in up_pair], axis=1).astype(f32)
    grad_qkv_w = jnp.concatenate(q_pair, axis=1).astype(f32)
    return (
        layer_out,
        grad_tokens,
        grad_qkv_w,
        owned[4],
        owned[5],
        grad_proj_w,
        owned[0],
        owned[6],
        owned[7],
        owned[1],
        owned[2],
        grad_up_w,
        owned_up,
        grad_down_w,
        owned[3],
    )


def solution(mesh):
    rep, shard = mesh.shape["rep"], mesh.shape["shard"]
    rep_bits = tuple(f"r{i}" for i in range(rep.bit_length() - 1))
    shard_bits = tuple(f"s{i}" for i in range(shard.bit_length() - 1))
    fine = Mesh(mesh.devices.reshape((2,) * (len(rep_bits) + len(shard_bits))), rep_bits + shard_bits)
    every = P(rep_bits + shard_bits, None, None)
    matrix = P(shard_bits, None)
    vector = P(shard_bits)
    return jax.shard_map(
        functools.partial(per_device, rep_bits, shard_bits),
        mesh=fine,
        in_specs=(
            every,
            P(rep_bits + shard_bits),
            matrix,
            vector,
            vector,
            matrix,
            vector,
            vector,
            vector,
            vector,
            vector,
            matrix,
            vector,
            matrix,
            vector,
            every,
        ),
        out_specs=(
            every,
            every,
            matrix,
            vector,
            vector,
            matrix,
            vector,
            vector,
            vector,
            vector,
            vector,
            matrix,
            vector,
            matrix,
            vector,
        ),
        check_vma=False,
    )
```

```python
import functools
import math

import jax
import jax.numpy as jnp
from jax import lax
from jax.experimental import pallas as pl
from jax.experimental.pallas import tpu as pltpu
from jax.sharding import Mesh, PartitionSpec as P

H = 12
HD = 64
EPSILON = 1e-06
ROOT_HALF = 1.0 / math.sqrt(2.0)
INV_ROOT_TAU = 1.0 / math.sqrt(2.0 * math.pi)
f32 = jnp.float32
bf16 = jnp.bfloat16
SWAP = [(0, 1), (1, 0)]
FREE = pl.CostEstimate(flops=0, bytes_accessed=0, transcendentals=0)


def norm_parts(values_in):
    row_mean = jnp.mean(values_in, axis=-1, keepdims=True)
    centred = values_in - row_mean
    inverse = lax.rsqrt(jnp.mean(centred * centred, axis=-1, keepdims=True) + EPSILON)
    return (centred * inverse, inverse)


def norm_back(grad_normal, normal_rows, inverse_rows):
    first_mean = jnp.mean(grad_normal, axis=-1, keepdims=True)
    second_mean = jnp.mean(grad_normal * normal_rows, axis=-1, keepdims=True)
    return inverse_rows * (grad_normal - first_mean - normal_rows * second_mean)


def dot_nt(a, b):
    return lax.dot_general(a, b, (((1,), (1,)), ((), ())), preferred_element_type=f32)


def dot_tn(a, b):
    return lax.dot_general(a, b, (((0,), (0,)), ((), ())), preferred_element_type=f32)


def dot_nn(a, b):
    return jnp.dot(a, b, preferred_element_type=f32)


def attention_kernel(length, qkv_ref, out_ref, prob_ref):
    rows = qkv_ref.shape[1]
    width = H * HD
    first = lax.broadcasted_iota(jnp.int32, (1, 2 * HD), 1) < HD
    key_live = lax.broadcasted_iota(jnp.int32, (rows, 1), 0) < length
    for pair in range(H // 2):
        lanes = pl.ds(pair * 2 * HD, 2 * HD)
        q2 = qkv_ref[0, :, pl.ds(pair * 2 * HD, 2 * HD)] * jnp.asarray(HD ** (-0.5), bf16)
        k2 = qkv_ref[0, :, pl.ds(width + pair * 2 * HD, 2 * HD)]
        v2 = qkv_ref[0, :, pl.ds(2 * width + pair * 2 * HD, 2 * HD)]
        total = None
        for half in range(2):
            mask = first if half == 0 else jnp.logical_not(first)
            scores = dot_nt(jnp.where(mask, k2, jnp.zeros_like(k2)), q2)
            scores = jnp.where(key_live, scores, -1e30)
            expo = jnp.exp(scores - jnp.max(scores, axis=0, keepdims=True))
            probs = (expo * (1.0 / jnp.sum(expo, axis=0, keepdims=True))).astype(bf16)
            prob_ref[0, 2 * pair + half] = probs
            part = dot_tn(probs, jnp.where(mask, v2, jnp.zeros_like(v2)))
            total = part if total is None else total + part
        out_ref[0, :, lanes] = total.astype(bf16)


def attention_back_kernel(qkv_ref, prob_ref, grad_ref, out_ref, sums_ref):
    width = H * HD
    first = lax.broadcasted_iota(jnp.int32, (1, 2 * HD), 1) < HD
    scale = jnp.asarray(HD ** (-0.5), f32)

    @pl.when(pl.program_id(0) == 0)
    def _():
        sums_ref[...] = jnp.zeros_like(sums_ref)

    for pair in range(H // 2):
        spots = [pl.ds(part * width + pair * 2 * HD, 2 * HD) for part in range(3)]
        q2 = qkv_ref[0, :, spots[0]]
        k2 = qkv_ref[0, :, spots[1]]
        v2 = qkv_ref[0, :, spots[2]]
        g2 = grad_ref[0, :, spots[0]]
        totals = [None, None, None]
        for half in range(2):
            mask = first if half == 0 else jnp.logical_not(first)

            def keep(v):
                return jnp.where(mask, v, jnp.zeros_like(v))

            probs = prob_ref[0, 2 * pair + half]
            g_half = keep(g2)
            grad_probs = dot_nt(v2, g_half)
            probs_wide = probs.astype(f32)
            delta = jnp.sum(grad_probs * probs_wide, axis=0, keepdims=True)
            grad_scores = (probs_wide * (grad_probs - delta)).astype(bf16)
            parts = (
                dot_tn(grad_scores, keep(k2)),
                dot_nn(grad_scores, keep(q2)),
                dot_nn(probs, g_half),
            )
            totals = [p if t is None else t + p for t, p in zip(totals, parts)]
        for part in range(3):
            value = totals[part] if part == 2 else totals[part] * scale
            value = value.astype(bf16)
            out_ref[0, :, spots[part]] = value
            sums_ref[:, spots[part]] += jnp.sum(value.astype(f32), axis=0, keepdims=True)


def stay(value):
    return pltpu.with_memory_space_constraint(value, pltpu.HBM)


def attention(qkv, length):
    slots, rows, wide = qkv.shape
    width = wide // 3
    return pl.pallas_call(
        functools.partial(attention_kernel, length),
        grid=(slots,),
        in_specs=[pl.BlockSpec((1, rows, wide), lambda i: (i, 0, 0))],
        out_specs=[
            pl.BlockSpec((1, rows, width), lambda i: (i, 0, 0)),
            pl.BlockSpec((1, H, rows, rows), lambda i: (i, 0, 0, 0)),
        ],
        out_shape=[
            jax.ShapeDtypeStruct((slots, rows, width), bf16),
            pltpu.HBM((slots, H, rows, rows), bf16),
        ],
        compiler_params=pltpu.CompilerParams(vmem_limit_bytes=28 * 2**20),
        cost_estimate=FREE,
        name="attention",
    )(qkv)


def attention_back(qkv, probs, grad):
    slots, rows, wide = qkv.shape
    width = wide // 3
    return pl.pallas_call(
        attention_back_kernel,
        grid=(slots,),
        in_specs=[
            pl.BlockSpec((1, rows, wide), lambda i: (i, 0, 0)),
            pl.BlockSpec((1, H, rows, rows), lambda i: (i, 0, 0, 0)),
            pl.BlockSpec((1, rows, width), lambda i: (i, 0, 0)),
        ],
        out_specs=[
            pl.BlockSpec((1, rows, wide), lambda i: (i, 0, 0)),
            pl.BlockSpec((1, wide), lambda i: (0, 0)),
        ],
        out_shape=[
            jax.ShapeDtypeStruct((slots, rows, wide), bf16),
            jax.ShapeDtypeStruct((1, wide), f32),
        ],
        compiler_params=pltpu.CompilerParams(vmem_limit_bytes=28 * 2**20),
        cost_estimate=FREE,
        name="attention_back",
    )(qkv, stay(probs), grad)


def hidden_back_kernel(grad_ref, weight_ref, slope_ref, out_ref, sums_ref):
    grad = dot_nt(grad_ref[...], weight_ref[...]) * slope_ref[...].astype(f32)
    grad = grad.astype(bf16)
    out_ref[...] = grad
    sums_ref[...] = jnp.sum(grad.astype(f32), axis=0, keepdims=True)


def hidden_back(grad, weight, slope):
    rows, width = grad.shape
    wide = weight.shape[0]
    tile = 512
    return pl.pallas_call(
        hidden_back_kernel,
        grid=(wide // tile,),
        in_specs=[
            pl.BlockSpec((rows, width), lambda i: (0, 0)),
            pl.BlockSpec((tile, width), lambda i: (i, 0)),
            pl.BlockSpec((rows, tile), lambda i: (0, i)),
        ],
        out_specs=[
            pl.BlockSpec((rows, tile), lambda i: (0, i)),
            pl.BlockSpec((1, tile), lambda i: (0, i)),
        ],
        out_shape=[
            pltpu.HBM((rows, wide), bf16),
            jax.ShapeDtypeStruct((1, wide), f32),
        ],
        compiler_params=pltpu.CompilerParams(vmem_limit_bytes=28 * 2**20),
        cost_estimate=FREE,
        name="hidden_back",
    )(grad, weight, slope)


def norm_back_kernel(grad_ref, weight_ref, value_ref, gain_ref, past_ref, out_ref, low_ref, sums_ref):
    upstream = dot_nt(grad_ref[...], weight_ref[...])
    normal, inverse = norm_parts(value_ref[...].astype(f32))

    @pl.when(pl.program_id(0) == 0)
    def _():
        sums_ref[...] = jnp.zeros_like(sums_ref)

    sums_ref[0:1] += jnp.sum(upstream * normal, axis=0, keepdims=True)
    sums_ref[1:2] += jnp.sum(upstream, axis=0, keepdims=True)
    total = past_ref[...].astype(f32) + norm_back(upstream * gain_ref[...], normal, inverse)
    low = total.astype(bf16)
    out_ref[...] = total
    low_ref[...] = low
    sums_ref[2:3] += jnp.sum(low.astype(f32), axis=0, keepdims=True)


def norm_back_low_kernel(grad_ref, weight_ref, value_ref, gain_ref, past_ref, low_ref, sums_ref):
    upstream = dot_nt(grad_ref[...], weight_ref[...])
    normal, inverse = norm_parts(value_ref[...].astype(f32))

    @pl.when(pl.program_id(0) == 0)
    def _():
        sums_ref[...] = jnp.zeros_like(sums_ref)

    sums_ref[0:1] += jnp.sum(upstream * normal, axis=0, keepdims=True)
    sums_ref[1:2] += jnp.sum(upstream, axis=0, keepdims=True)
    total = past_ref[...].astype(f32) + norm_back(upstream * gain_ref[...], normal, inverse)
    low_ref[...] = total.astype(bf16)


def matmul_norm_back(grad, weight, values, gain, past, count, both):
    rows, wide = grad.shape
    width = weight.shape[0]
    tile = rows // count
    tall = pl.BlockSpec((tile, width), lambda i: (i, 0))
    outs = [jax.ShapeDtypeStruct((rows, width), f32)] if both else []
    outs += [jax.ShapeDtypeStruct((rows, width), bf16), jax.ShapeDtypeStruct((8, width), f32)]
    return pl.pallas_call(
        norm_back_kernel if both else norm_back_low_kernel,
        grid=(count,),
        in_specs=[
            pl.BlockSpec((tile, wide), lambda i: (i, 0)),
            pl.BlockSpec((width, wide), lambda i: (0, 0)),
            tall,
            pl.BlockSpec((1, width), lambda i: (0, 0)),
            tall,
        ],
        out_specs=[tall] * (len(outs) - 1) + [pl.BlockSpec((8, width), lambda i: (0, 0))],
        out_shape=outs,
        compiler_params=pltpu.CompilerParams(vmem_limit_bytes=28 * 2**20),
        cost_estimate=FREE,
        name="matmul_norm_back",
    )(*map(stay if both else (lambda v: v), (grad, weight, values)), gain.reshape(1, width), past)


class Net:
    def __init__(self, rep_bits, shard_bits):
        self.core, self.x, self.y = rep_bits[-1], rep_bits[-2], rep_bits[-3]
        self.extra = tuple(rep_bits[:-3])
        self.rep = tuple(rep_bits)
        self.shard = tuple(shard_bits)
        self.bit = {name: lax.axis_index(name) for name in self.rep + self.shard}

    def other_way(self, name):
        return self.y if name == self.x else self.x

    def swap(self, piece, name):
        return lax.ppermute(piece, name, SWAP)

    def place(self, mine, other, name):
        bit = self.bit[name]
        return jnp.where(bit == 0, mine, other), jnp.where(bit == 0, other, mine)

    def join(self, piece, other, name, spot):
        return jnp.stack(self.place(piece, other, name), axis=spot)

    def grow(self, piece, name, spot):
        return self.join(piece, self.swap(piece, name), name, spot)

    def part_with(self, piece, name, spot):
        bit = self.bit[name]
        send = lax.dynamic_index_in_dim(piece, 1 - bit, spot, keepdims=False)
        keep = lax.dynamic_index_in_dim(piece, bit, spot, keepdims=False)
        return keep, self.swap(send, name)

    def core_half(self, matrix, other=False):
        half = matrix.shape[1] // 2
        bit = self.bit[self.core]
        return lax.dynamic_slice_in_dim(matrix, ((1 - bit) if other else bit) * half, half, 1)

    def both_cores(self, piece):
        return self.place(piece, self.swap(piece, self.core), self.core)

    def row_half(self, matrix, name):
        rows = matrix.shape[0] // 2
        return lax.dynamic_slice_in_dim(matrix, self.bit[name] * rows, rows, 0)

    def group_up(self, values):
        for spot, name in enumerate(self.shard):
            values = self.grow(values, name, spot)
        return values

    def place_in_group(self):
        me = 0
        for name in self.shard:
            me = 2 * me + self.bit[name]
        return me


def add(pair):
    return (pair[0].astype(f32) + pair[1].astype(f32)).astype(bf16)


def together(*values):
    return lax.optimization_barrier(values)


def cut_of(columns):
    return -(-columns // 256) * 128


def per_device(
    rep_bits,
    shard_bits,
    tokens,
    counts,
    w_qkv,
    b_query,
    b_value,
    w_proj,
    b_proj,
    gain_one,
    bias_one,
    gain_two,
    bias_two,
    w_up,
    b_up,
    w_down,
    b_down,
    out_grad,
):
    net = Net(rep_bits, shard_bits)
    group = 2 ** len(shard_bits)
    slot_count, length, width = tokens.shape
    padded = -(-length // 16) * 16
    row_count = slot_count * padded
    wide = w_up.shape[1]
    part = width // group
    blocks = w_down.shape[0] // part
    fill = ((0, 0), (0, padded - length), (0, 0))
    far, near = net.shard
    half_up, half_mid = wide // 2, width // 2

    plane = (net.x, net.y)

    def ways(piece):
        cut = cut_of(piece.shape[-1])
        return [piece[..., :cut], piece[..., cut:]]

    def fetch(mine):
        return jnp.concatenate(
            [net.row_half(p, name) for p, name in zip(ways(mine), plane)], axis=1
        )

    def send_plane(piece):
        return [net.swap(p, name) for p, name in zip(ways(piece), plane)]

    def join_plane(piece, others, spot):
        pairs = zip(ways(piece), others, plane)
        return jnp.concatenate(
            [net.join(p, o, name, spot).reshape(-1, p.shape[-1]) for p, o, name in pairs], axis=1
        )

    small = jnp.stack(
        [b_query, b_value, b_proj, gain_one, bias_one, gain_two, bias_two, b_down]
    )
    small = jnp.concatenate([small, b_up.reshape(-1, part)], axis=0)
    q_way = net.grow(fetch(net.core_half(w_qkv)), far, 0)
    small = net.grow(small, far, 0)
    mid_way = fetch(jnp.concatenate([net.core_half(w_up), net.core_half(w_proj)], axis=1))
    q_way, small = together(q_way, small)
    q_way = net.grow(q_way, near, 1)
    small = net.grow(small, near, 1)
    down_mine = net.core_half(w_down).reshape(blocks, part, half_mid)
    down_mine = jnp.concatenate([down_mine[i] for i in range(blocks)], axis=1)
    q_way, small, mid_way, down_mine, tokens = together(
        q_way, small, mid_way, down_mine, tokens
    )
    q_got = send_plane(q_way)
    mid_got = net.swap(mid_way, far)
    small = small.astype(f32).reshape(group, -1, part)
    rows = small[:, :8].transpose(1, 0, 2).reshape(8, width)
    query_bias, value_bias, proj_bias, gain_1, bias_1, gain_2, bias_2, down_bias = (
        rows[i] for i in range(8)
    )
    up_bias = small[:, 8:].reshape(wide)
    q_way, *q_got = together(q_way, *q_got)
    q_way, mid_way, down_way = together(join_plane(q_way, q_got, 2), mid_way, fetch(down_mine))
    qkv_pair = net.both_cores(q_way)
    mid_way = net.join(mid_way, mid_got, far, 0)
    mid_got = net.swap(mid_way, near)
    (qkv_full,) = together(jnp.concatenate(qkv_pair, axis=1))

    live_slots = (jnp.arange(slot_count, dtype=jnp.int32) < counts[0]).astype(f32)
    live_rows = jnp.repeat(live_slots, padded)[:, None]
    low_inputs = jnp.pad(tokens, fill).reshape(row_count, width)
    inputs = low_inputs.astype(f32)
    normal_one, inverse_one = norm_parts(inputs)
    normed_one = (normal_one * gain_1 + bias_1).astype(bf16)
    qkv_bias = jnp.concatenate([query_bias, jnp.zeros_like(query_bias), value_bias])
    joined = (dot_nn(normed_one, qkv_full) + qkv_bias).astype(bf16)
    joined = joined.reshape(slot_count, padded, 3 * width)
    mixed, probs = attention(joined, length)
    mixed, mid_way, mid_got, down_way = together(mixed, mid_way, mid_got, down_way)
    mid_way = net.join(mid_way, mid_got, near, 1)
    mixed, mid_way, down_way = together(mixed, mid_way, down_way)
    mid_got = send_plane(mid_way)
    down_got = net.swap(down_way, far)
    mixed, mid_way, down_way, out_grad, down_got, *mid_got = together(
        mixed, mid_way, down_way, out_grad, down_got, *mid_got
    )
    down_way = net.join(down_way, down_got, far, 0)
    mid_way, down_way = together(join_plane(mid_way, mid_got, 2), down_way)
    down_got = net.swap(down_way, near)
    *mid_pairs, down_way = together(*net.both_cores(mid_way), down_way)
    down_way = net.join(down_way, down_got, near, 1)
    down_got = send_plane(down_way)
    mixed = mixed.reshape(row_count, width)
    mid = mid_pairs
    up_full = jnp.concatenate([m[:, :half_up] for m in mid], axis=1)
    proj_full = jnp.concatenate([m[:, half_up:] for m in mid], axis=1)
    up_full, proj_full = together(up_full, proj_full)
    middle = inputs + (dot_nn(mixed, proj_full) + proj_bias)
    normal_two, inverse_two = norm_parts(middle)
    normed_two = (normal_two * gain_2 + bias_2).astype(bf16)
    hidden = dot_nn(normed_two, up_full) + up_bias
    share = 0.5 * (1.0 + lax.erf(hidden * ROOT_HALF))
    active = (hidden * share).astype(bf16)
    active, down_way = together(active, down_way)
    down_pairs = net.both_cores(join_plane(down_way, down_got, 2))
    slope = (share + hidden * jnp.exp(-0.5 * hidden * hidden) * INV_ROOT_TAU).astype(bf16)
    down = [
        jnp.stack(
            [
                d.reshape(group, part, -1)[:, :, b * half_mid : (b + 1) * half_mid]
                for b in range(blocks)
            ],
            axis=1,
        )
        for d in down_pairs
    ]
    (down_full,) = together(jnp.concatenate(down, axis=3).reshape(wide, width))

    def start_sum(left, right):
        return dot_tn(left, net.core_half(right, True)).astype(bf16)

    def own_sum(left, right, other):
        total = dot_tn(left, net.core_half(right)) + other.astype(f32)
        total = total.astype(bf16)
        return total.reshape(2, 2, 2, -1, total.shape[1])

    def part_plane(piece):
        pairs = [net.part_with(p, name, 2) for p, name in zip(ways(piece), plane)]
        return [p[0] for p in pairs], [p[1] for p in pairs]

    def add_plane(keeps, others):
        return jnp.concatenate([add(pair) for pair in zip(keeps, others)], axis=-1)

    def exchange_plane(piece):
        done = []
        for p, name in zip(ways(piece), plane):
            for other in (net.other_way(name),) + net.extra:
                p = add((p, net.swap(p, other)))
            done.append(p)
        return done

    def grow_plane(pieces):
        return jnp.concatenate(
            [
                net.grow(p, name, 0).reshape(-1, p.shape[-1])
                for p, name in zip(pieces, plane)
            ],
            axis=1,
        )

    grad_branch = jnp.pad(out_grad, fill).reshape(row_count, width)
    grad_branch = grad_branch * live_rows.astype(bf16)
    branch_2, d_send = together(grad_branch, start_sum(active, grad_branch))
    d_other = net.swap(d_send, net.core)
    result = middle + (dot_nn(active, down_full) + down_bias)
    layer_out = (result * live_rows).astype(bf16)
    layer_out = layer_out.reshape(slot_count, padded, width)[:, :length]
    branch_3, layer_out = together(grad_branch, layer_out)
    d_piece = own_sum(active, branch_3, d_other)
    branch_2, d_piece = together(branch_2, d_piece)
    fine = d_piece.shape[3] // 2
    d_pairs = [
        net.part_with(d_piece[:, :, :, i * fine : (i + 1) * fine], name, 2)
        for i, name in enumerate(plane)
    ]
    d_keeps, d_others = [p[0] for p in d_pairs], [p[1] for p in d_pairs]
    grad_hidden, up_sums = hidden_back(branch_2, down_full, slope)
    grad_hidden, u_send = together(grad_hidden, start_sum(normed_two, grad_hidden))
    u_other = net.swap(u_send, net.core)
    grad_middle, grad_attn, mid_sums = matmul_norm_back(
        grad_hidden, up_full, middle, gain_2, grad_branch, slot_count, True
    )
    grad_attn, d_1, d_2, o_1, o_2 = together(grad_attn, *d_keeps, *d_others)
    grad_hidden, grad_attn = together(grad_hidden, grad_attn)
    grad_attn, p_send = together(grad_attn, start_sum(mixed, grad_attn))
    p_other = net.swap(p_send, net.core)
    u_piece = own_sum(normed_two, grad_hidden, u_other)
    grad_attn, u_piece = together(grad_attn, u_piece)
    p_piece = own_sum(mixed, grad_attn, p_other)
    u_piece = jnp.concatenate([u_piece, p_piece], axis=-1)
    grad_attn_2, u_piece, d_1, d_2, o_1, o_2 = together(grad_attn, u_piece, d_1, d_2, o_1, o_2)
    d_piece = add_plane([d_1, d_2], [o_1, o_2])
    d_pair = net.part_with(d_piece, near, 1)
    u_keeps, u_others = part_plane(u_piece)
    grad_mixed = dot_nt(grad_attn_2, proj_full).astype(bf16)
    grad_joined, joined_sums = attention_back(
        joined, probs, grad_mixed.reshape(slot_count, padded, width)
    )
    grad_joined, d_keep, d_other, u_1, u_2, o_1, o_2 = together(
        grad_joined.reshape(row_count, 3 * width), *d_pair, *u_keeps, *u_others
    )
    grad_joined, q_send, d_keep, d_other, u_1, u_2, o_1, o_2 = together(
        grad_joined, start_sum(normed_one, grad_joined), d_keep, d_other, u_1, u_2, o_1, o_2
    )
    q_other = net.swap(q_send, net.core)
    u_piece = add_plane([u_1, u_2], [o_1, o_2])
    d_piece = add((d_keep, d_other))
    grad_joined, d_piece, u_piece = together(grad_joined, d_piece, u_piece)
    u_pair = net.part_with(u_piece, near, 1)
    d_pair = net.part_with(d_piece, far, 0)
    q_piece = own_sum(normed_one, grad_joined, q_other)
    grad_joined, q_piece = together(grad_joined, q_piece)
    q_keeps, q_others = part_plane(q_piece)
    grad_tokens, first_sums = matmul_norm_back(
        grad_joined, qkv_full, low_inputs, gain_1, grad_middle, slot_count, False
    )
    grad_tokens = grad_tokens.reshape(slot_count, padded, width)[:, :length]

    first_sums, u_keep, u_other, d_keep, d_other, q_1, q_2, o_1, o_2 = together(
        first_sums, *u_pair, *d_pair, *q_keeps, *q_others
    )
    q_piece = add_plane([q_1, q_2], [o_1, o_2])
    u_piece = add((u_keep, u_other))
    q_piece, u_piece, first_sums, d_keep, branch_4 = together(
        q_piece, u_piece, first_sums, d_keep, grad_branch
    )
    q_pair = net.part_with(q_piece, near, 1)
    u_pair = net.part_with(u_piece, far, 0)
    grad_down_b = jnp.sum(branch_4.astype(f32), axis=0, keepdims=True)
    vectors = [
        mid_sums[2:3],
        mid_sums[0:2],
        grad_down_b,
        joined_sums[:, :width],
        joined_sums[:, 2 * width :],
        first_sums[0:2],
    ]
    vectors += [up_sums[:, k * width : (k + 1) * width] for k in range(group)]
    vectors = jnp.concatenate(vectors, axis=0)
    sums = vectors + net.swap(vectors, net.core)
    d_piece = exchange_plane(add((d_keep, d_other)))
    q_keep, q_other, u_keep, u_other, sums, *d_piece = together(*q_pair, *u_pair, sums, *d_piece)
    q_piece = add((q_keep, q_other))
    u_piece = add((u_keep, u_other))
    q_piece, u_piece, sums, *d_piece = together(q_piece, u_piece, sums, *d_piece)
    q_pair = net.part_with(q_piece, far, 0)
    u_piece = exchange_plane(u_piece)
    down_shard = jnp.stack(
        [net.grow(p, name, 0) for p, name in zip(d_piece, plane)], axis=1
    ).reshape(-1, half_mid)
    sums = sums + net.swap(sums, net.x)
    q_keep, q_other, sums, down_shard, *u_piece = together(*q_pair, sums, down_shard, *u_piece)
    q_1, q_2 = exchange_plane(add((q_keep, q_other)))
    up_shard = grow_plane(u_piece)
    down_pair = net.both_cores(down_shard)
    sums = sums + net.swap(sums, net.y)
    grad_down_w = jnp.concatenate(down_pair, axis=1).astype(f32)
    q_1, q_2, sums, up_shard, grad_down_w = together(q_1, q_2, sums, up_shard, grad_down_w)
    q_piece = grow_plane([q_1, q_2])
    up_pair = net.both_cores(up_shard)
    sums = sums + net.swap(sums, far)
    q_piece, sums, *up_pair = together(q_piece, sums, *up_pair)
    q_pair = net.both_cores(q_piece)
    for name in (near,) + net.extra:
        sums = sums + net.swap(sums, name)
    me = net.place_in_group()
    owned = lax.dynamic_slice_in_dim(sums[:8], me * part, part, 1)
    owned_up = lax.dynamic_index_in_dim(sums, 8 + me, 0, keepdims=False)
    grad_up_w = jnp.concatenate([p[:, :half_up] for p in up_pair], axis=1).astype(f32)
    grad_proj_w = jnp.concatenate([p[:, half_up:] for p in up_pair], axis=1).astype(f32)
    grad_qkv_w = jnp.concatenate(q_pair, axis=1).astype(f32)
    return (
        layer_out,
        grad_tokens,
        grad_qkv_w,
        owned[4],
        owned[5],
        grad_proj_w,
        owned[0],
        owned[6],
        owned[7],
        owned[1],
        owned[2],
        grad_up_w,
        owned_up,
        grad_down_w,
        owned[3],
    )


def solution(mesh):
    rep, shard = mesh.shape["rep"], mesh.shape["shard"]
    rep_bits = tuple(f"r{i}" for i in range(rep.bit_length() - 1))
    shard_bits = tuple(f"s{i}" for i in range(shard.bit_length() - 1))
    fine = Mesh(mesh.devices.reshape((2,) * (len(rep_bits) + len(shard_bits))), rep_bits + shard_bits)
    every = P(rep_bits + shard_bits, None, None)
    matrix = P(shard_bits, None)
    vector = P(shard_bits)
    return jax.shard_map(
        functools.partial(per_device, rep_bits, shard_bits),
        mesh=fine,
        in_specs=(
            every,
            P(rep_bits + shard_bits),
            matrix,
            vector,
            vector,
            matrix,
            vector,
            vector,
            vector,
            vector,
            vector,
            matrix,
            vector,
            matrix,
            vector,
            every,
        ),
        out_specs=(
            every,
            every,
            matrix,
            vector,
            vector,
            matrix,
            vector,
            vector,
            vector,
            vector,
            vector,
            matrix,
            vector,
            matrix,
            vector,
        ),
        check_vma=False,
    )
```

```python
import functools
import math

import jax
import jax.numpy as jnp
from jax import lax
from jax.experimental import pallas as pl
from jax.experimental.pallas import tpu as pltpu
from jax.sharding import Mesh, PartitionSpec as P

H = 12
HD = 64
EPSILON = 1e-06
ROOT_HALF = 1.0 / math.sqrt(2.0)
INV_ROOT_TAU = 1.0 / math.sqrt(2.0 * math.pi)
f32 = jnp.float32
bf16 = jnp.bfloat16
SWAP = [(0, 1), (1, 0)]
FREE = pl.CostEstimate(flops=0, bytes_accessed=0, transcendentals=0)


def norm_parts(values_in):
    row_mean = jnp.mean(values_in, axis=-1, keepdims=True)
    centred = values_in - row_mean
    inverse = lax.rsqrt(jnp.mean(centred * centred, axis=-1, keepdims=True) + EPSILON)
    return (centred * inverse, inverse)


def norm_back(grad_normal, normal_rows, inverse_rows):
    first_mean = jnp.mean(grad_normal, axis=-1, keepdims=True)
    second_mean = jnp.mean(grad_normal * normal_rows, axis=-1, keepdims=True)
    return inverse_rows * (grad_normal - first_mean - normal_rows * second_mean)


def dot_nt(a, b):
    return lax.dot_general(a, b, (((1,), (1,)), ((), ())), preferred_element_type=f32)


def dot_tn(a, b):
    return lax.dot_general(a, b, (((0,), (0,)), ((), ())), preferred_element_type=f32)


def dot_nn(a, b):
    return jnp.dot(a, b, preferred_element_type=f32)


def attention_kernel(length, qkv_ref, out_ref, prob_ref):
    rows = qkv_ref.shape[1]
    width = H * HD
    first = lax.broadcasted_iota(jnp.int32, (1, 2 * HD), 1) < HD
    key_live = lax.broadcasted_iota(jnp.int32, (rows, 1), 0) < length
    for pair in range(H // 2):
        lanes = pl.ds(pair * 2 * HD, 2 * HD)
        q2 = qkv_ref[0, :, pl.ds(pair * 2 * HD, 2 * HD)] * jnp.asarray(HD ** (-0.5), bf16)
        k2 = qkv_ref[0, :, pl.ds(width + pair * 2 * HD, 2 * HD)]
        v2 = qkv_ref[0, :, pl.ds(2 * width + pair * 2 * HD, 2 * HD)]
        total = None
        for half in range(2):
            mask = first if half == 0 else jnp.logical_not(first)
            scores = dot_nt(jnp.where(mask, k2, jnp.zeros_like(k2)), q2)
            scores = jnp.where(key_live, scores, -1e30)
            expo = jnp.exp(scores - jnp.max(scores, axis=0, keepdims=True))
            probs = (expo * (1.0 / jnp.sum(expo, axis=0, keepdims=True))).astype(bf16)
            prob_ref[0, 2 * pair + half] = probs
            part = dot_tn(probs, jnp.where(mask, v2, jnp.zeros_like(v2)))
            total = part if total is None else total + part
        out_ref[0, :, lanes] = total.astype(bf16)


def attention_back_kernel(qkv_ref, prob_ref, grad_ref, out_ref, sums_ref):
    width = H * HD
    first = lax.broadcasted_iota(jnp.int32, (1, 2 * HD), 1) < HD
    scale = jnp.asarray(HD ** (-0.5), f32)

    @pl.when(pl.program_id(0) == 0)
    def _():
        sums_ref[...] = jnp.zeros_like(sums_ref)

    for pair in range(H // 2):
        spots = [pl.ds(part * width + pair * 2 * HD, 2 * HD) for part in range(3)]
        q2 = qkv_ref[0, :, spots[0]]
        k2 = qkv_ref[0, :, spots[1]]
        v2 = qkv_ref[0, :, spots[2]]
        g2 = grad_ref[0, :, spots[0]]
        totals = [None, None, None]
        for half in range(2):
            mask = first if half == 0 else jnp.logical_not(first)

            def keep(v):
                return jnp.where(mask, v, jnp.zeros_like(v))

            probs = prob_ref[0, 2 * pair + half]
            g_half = keep(g2)
            grad_probs = dot_nt(v2, g_half)
            probs_wide = probs.astype(f32)
            delta = jnp.sum(grad_probs * probs_wide, axis=0, keepdims=True)
            grad_scores = (probs_wide * (grad_probs - delta)).astype(bf16)
            parts = (
                dot_tn(grad_scores, keep(k2)),
                dot_nn(grad_scores, keep(q2)),
                dot_nn(probs, g_half),
            )
            totals = [p if t is None else t + p for t, p in zip(totals, parts)]
        for part in range(3):
            value = totals[part] if part == 2 else totals[part] * scale
            value = value.astype(bf16)
            out_ref[0, :, spots[part]] = value
            sums_ref[:, spots[part]] += jnp.sum(value.astype(f32), axis=0, keepdims=True)


def stay(value):
    return pltpu.with_memory_space_constraint(value, pltpu.HBM)


def attention(qkv, length):
    slots, rows, wide = qkv.shape
    width = wide // 3
    return pl.pallas_call(
        functools.partial(attention_kernel, length),
        grid=(slots,),
        in_specs=[pl.BlockSpec((1, rows, wide), lambda i: (i, 0, 0))],
        out_specs=[
            pl.BlockSpec((1, rows, width), lambda i: (i, 0, 0)),
            pl.BlockSpec((1, H, rows, rows), lambda i: (i, 0, 0, 0)),
        ],
        out_shape=[
            jax.ShapeDtypeStruct((slots, rows, width), bf16),
            pltpu.HBM((slots, H, rows, rows), bf16),
        ],
        compiler_params=pltpu.CompilerParams(vmem_limit_bytes=28 * 2**20),
        cost_estimate=FREE,
        name="attention",
    )(qkv)


def attention_back(qkv, probs, grad):
    slots, rows, wide = qkv.shape
    width = wide // 3
    return pl.pallas_call(
        attention_back_kernel,
        grid=(slots,),
        in_specs=[
            pl.BlockSpec((1, rows, wide), lambda i: (i, 0, 0)),
            pl.BlockSpec((1, H, rows, rows), lambda i: (i, 0, 0, 0)),
            pl.BlockSpec((1, rows, width), lambda i: (i, 0, 0)),
        ],
        out_specs=[
            pl.BlockSpec((1, rows, wide), lambda i: (i, 0, 0)),
            pl.BlockSpec((1, wide), lambda i: (0, 0)),
        ],
        out_shape=[
            jax.ShapeDtypeStruct((slots, rows, wide), bf16),
            jax.ShapeDtypeStruct((1, wide), f32),
        ],
        compiler_params=pltpu.CompilerParams(vmem_limit_bytes=28 * 2**20),
        cost_estimate=FREE,
        name="attention_back",
    )(qkv, stay(probs), grad)


def hidden_back_kernel(grad_ref, weight_ref, slope_ref, out_ref, sums_ref):
    grad = dot_nt(grad_ref[...], weight_ref[...]) * slope_ref[...].astype(f32)
    grad = grad.astype(bf16)
    out_ref[...] = grad
    sums_ref[...] = jnp.sum(grad.astype(f32), axis=0, keepdims=True)


def hidden_back(grad, weight, slope):
    rows, width = grad.shape
    wide = weight.shape[0]
    tile = 512
    return pl.pallas_call(
        hidden_back_kernel,
        grid=(wide // tile,),
        in_specs=[
            pl.BlockSpec((rows, width), lambda i: (0, 0)),
            pl.BlockSpec((tile, width), lambda i: (i, 0)),
            pl.BlockSpec((rows, tile), lambda i: (0, i)),
        ],
        out_specs=[
            pl.BlockSpec((rows, tile), lambda i: (0, i)),
            pl.BlockSpec((1, tile), lambda i: (0, i)),
        ],
        out_shape=[
            pltpu.HBM((rows, wide), bf16),
            jax.ShapeDtypeStruct((1, wide), f32),
        ],
        compiler_params=pltpu.CompilerParams(vmem_limit_bytes=28 * 2**20),
        cost_estimate=FREE,
        name="hidden_back",
    )(grad, weight, slope)


def norm_back_kernel(grad_ref, weight_ref, value_ref, gain_ref, past_ref, out_ref, low_ref, sums_ref):
    upstream = dot_nt(grad_ref[...], weight_ref[...])
    normal, inverse = norm_parts(value_ref[...].astype(f32))

    @pl.when(pl.program_id(0) == 0)
    def _():
        sums_ref[...] = jnp.zeros_like(sums_ref)

    sums_ref[0:1] += jnp.sum(upstream * normal, axis=0, keepdims=True)
    sums_ref[1:2] += jnp.sum(upstream, axis=0, keepdims=True)
    total = past_ref[...].astype(f32) + norm_back(upstream * gain_ref[...], normal, inverse)
    low = total.astype(bf16)
    out_ref[...] = total
    low_ref[...] = low
    sums_ref[2:3] += jnp.sum(low.astype(f32), axis=0, keepdims=True)


def norm_back_low_kernel(grad_ref, weight_ref, value_ref, gain_ref, past_ref, low_ref, sums_ref):
    upstream = dot_nt(grad_ref[...], weight_ref[...])
    normal, inverse = norm_parts(value_ref[...].astype(f32))

    @pl.when(pl.program_id(0) == 0)
    def _():
        sums_ref[...] = jnp.zeros_like(sums_ref)

    sums_ref[0:1] += jnp.sum(upstream * normal, axis=0, keepdims=True)
    sums_ref[1:2] += jnp.sum(upstream, axis=0, keepdims=True)
    total = past_ref[...].astype(f32) + norm_back(upstream * gain_ref[...], normal, inverse)
    low_ref[...] = total.astype(bf16)


def matmul_norm_back(grad, weight, values, gain, past, count, both):
    rows, wide = grad.shape
    width = weight.shape[0]
    tile = rows // count
    tall = pl.BlockSpec((tile, width), lambda i: (i, 0))
    outs = [jax.ShapeDtypeStruct((rows, width), f32)] if both else []
    outs += [jax.ShapeDtypeStruct((rows, width), bf16), jax.ShapeDtypeStruct((8, width), f32)]
    return pl.pallas_call(
        norm_back_kernel if both else norm_back_low_kernel,
        grid=(count,),
        in_specs=[
            pl.BlockSpec((tile, wide), lambda i: (i, 0)),
            pl.BlockSpec((width, wide), lambda i: (0, 0)),
            tall,
            pl.BlockSpec((1, width), lambda i: (0, 0)),
            tall,
        ],
        out_specs=[tall] * (len(outs) - 1) + [pl.BlockSpec((8, width), lambda i: (0, 0))],
        out_shape=outs,
        compiler_params=pltpu.CompilerParams(vmem_limit_bytes=28 * 2**20),
        cost_estimate=FREE,
        name="matmul_norm_back",
    )(*map(stay if both else (lambda v: v), (grad, weight)), values, gain.reshape(1, width), past)


class Net:
    def __init__(self, rep_bits, shard_bits):
        self.core, self.x, self.y = rep_bits[-1], rep_bits[-2], rep_bits[-3]
        self.extra = tuple(rep_bits[:-3])
        self.rep = tuple(rep_bits)
        self.shard = tuple(shard_bits)
        self.bit = {name: lax.axis_index(name) for name in self.rep + self.shard}

    def other_way(self, name):
        return self.y if name == self.x else self.x

    def swap(self, piece, name):
        return lax.ppermute(piece, name, SWAP)

    def place(self, mine, other, name):
        bit = self.bit[name]
        return jnp.where(bit == 0, mine, other), jnp.where(bit == 0, other, mine)

    def join(self, piece, other, name, spot):
        return jnp.stack(self.place(piece, other, name), axis=spot)

    def grow(self, piece, name, spot):
        return self.join(piece, self.swap(piece, name), name, spot)

    def part_with(self, piece, name, spot):
        bit = self.bit[name]
        send = lax.dynamic_index_in_dim(piece, 1 - bit, spot, keepdims=False)
        keep = lax.dynamic_index_in_dim(piece, bit, spot, keepdims=False)
        return keep, self.swap(send, name)

    def core_half(self, matrix, other=False):
        half = matrix.shape[1] // 2
        bit = self.bit[self.core]
        return lax.dynamic_slice_in_dim(matrix, ((1 - bit) if other else bit) * half, half, 1)

    def both_cores(self, piece):
        return self.place(piece, self.swap(piece, self.core), self.core)

    def row_half(self, matrix, name):
        rows = matrix.shape[0] // 2
        return lax.dynamic_slice_in_dim(matrix, self.bit[name] * rows, rows, 0)

    def group_up(self, values):
        for spot, name in enumerate(self.shard):
            values = self.grow(values, name, spot)
        return values

    def place_in_group(self):
        me = 0
        for name in self.shard:
            me = 2 * me + self.bit[name]
        return me


def add(pair):
    return (pair[0].astype(f32) + pair[1].astype(f32)).astype(bf16)


def together(*values):
    return lax.optimization_barrier(values)


def cut_of(columns):
    return -(-columns // 256) * 128


def per_device(
    rep_bits,
    shard_bits,
    tokens,
    counts,
    w_qkv,
    b_query,
    b_value,
    w_proj,
    b_proj,
    gain_one,
    bias_one,
    gain_two,
    bias_two,
    w_up,
    b_up,
    w_down,
    b_down,
    out_grad,
):
    net = Net(rep_bits, shard_bits)
    group = 2 ** len(shard_bits)
    slot_count, length, width = tokens.shape
    padded = -(-length // 16) * 16
    row_count = slot_count * padded
    wide = w_up.shape[1]
    part = width // group
    blocks = w_down.shape[0] // part
    fill = ((0, 0), (0, padded - length), (0, 0))
    far, near = net.shard
    half_up, half_mid = wide // 2, width // 2

    plane = (net.x, net.y)

    def ways(piece):
        cut = cut_of(piece.shape[-1])
        return [piece[..., :cut], piece[..., cut:]]

    def fetch(mine):
        return jnp.concatenate(
            [net.row_half(p, name) for p, name in zip(ways(mine), plane)], axis=1
        )

    def send_plane(piece):
        return [net.swap(p, name) for p, name in zip(ways(piece), plane)]

    def join_plane(piece, others, spot):
        pairs = zip(ways(piece), others, plane)
        return jnp.concatenate(
            [net.join(p, o, name, spot).reshape(-1, p.shape[-1]) for p, o, name in pairs], axis=1
        )

    small = jnp.stack(
        [b_query, b_value, b_proj, gain_one, bias_one, gain_two, bias_two, b_down]
    )
    small = jnp.concatenate([small, b_up.reshape(-1, part)], axis=0)
    q_way = net.grow(fetch(net.core_half(w_qkv)), far, 0)
    small = net.grow(small, far, 0)
    mid_way = fetch(jnp.concatenate([net.core_half(w_up), net.core_half(w_proj)], axis=1))
    q_way, small = together(q_way, small)
    q_way = net.grow(q_way, near, 1)
    small = net.grow(small, near, 1)
    down_mine = net.core_half(w_down).reshape(blocks, part, half_mid)
    down_mine = jnp.concatenate([down_mine[i] for i in range(blocks)], axis=1)
    q_way, small, mid_way, down_mine, tokens = together(
        q_way, small, mid_way, down_mine, tokens
    )
    q_got = send_plane(q_way)
    mid_got = net.swap(mid_way, far)
    small = small.astype(f32).reshape(group, -1, part)
    rows = small[:, :8].transpose(1, 0, 2).reshape(8, width)
    query_bias, value_bias, proj_bias, gain_1, bias_1, gain_2, bias_2, down_bias = (
        rows[i] for i in range(8)
    )
    up_bias = small[:, 8:].reshape(wide)
    q_way, *q_got = together(q_way, *q_got)
    q_way, mid_way, down_way = together(join_plane(q_way, q_got, 2), mid_way, fetch(down_mine))
    qkv_pair = net.both_cores(q_way)
    mid_way = net.join(mid_way, mid_got, far, 0)
    mid_got = net.swap(mid_way, near)
    (qkv_full,) = together(jnp.concatenate(qkv_pair, axis=1))

    live_slots = (jnp.arange(slot_count, dtype=jnp.int32) < counts[0]).astype(f32)
    live_rows = jnp.repeat(live_slots, padded)[:, None]
    low_inputs = jnp.pad(tokens, fill).reshape(row_count, width)
    inputs = low_inputs.astype(f32)
    normal_one, inverse_one = norm_parts(inputs)
    normed_one = (normal_one * gain_1 + bias_1).astype(bf16)
    qkv_bias = jnp.concatenate([query_bias, jnp.zeros_like(query_bias), value_bias])
    joined = (dot_nn(normed_one, qkv_full) + qkv_bias).astype(bf16)
    joined = joined.reshape(slot_count, padded, 3 * width)
    mixed, probs = attention(joined, length)
    mixed, mid_way, mid_got, down_way = together(mixed, mid_way, mid_got, down_way)
    mid_way = net.join(mid_way, mid_got, near, 1)
    mixed, mid_way, down_way = together(mixed, mid_way, down_way)
    mid_got = send_plane(mid_way)
    down_got = net.swap(down_way, far)
    mixed, mid_way, down_way, out_grad, down_got, *mid_got = together(
        mixed, mid_way, down_way, out_grad, down_got, *mid_got
    )
    down_way = net.join(down_way, down_got, far, 0)
    mid_way, down_way = together(join_plane(mid_way, mid_got, 2), down_way)
    down_got = net.swap(down_way, near)
    *mid_pairs, down_way = together(*net.both_cores(mid_way), down_way)
    down_way = net.join(down_way, down_got, near, 1)
    down_got = send_plane(down_way)
    mixed = mixed.reshape(row_count, width)
    mid = mid_pairs
    up_full = jnp.concatenate([m[:, :half_up] for m in mid], axis=1)
    proj_full = jnp.concatenate([m[:, half_up:] for m in mid], axis=1)
    up_full, proj_full = together(up_full, proj_full)
    middle = inputs + (dot_nn(mixed, proj_full) + proj_bias)
    normal_two, inverse_two = norm_parts(middle)
    normed_two = (normal_two * gain_2 + bias_2).astype(bf16)
    hidden = dot_nn(normed_two, up_full) + up_bias
    share = 0.5 * (1.0 + lax.erf(hidden * ROOT_HALF))
    active = (hidden * share).astype(bf16)
    active, down_way = together(active, down_way)
    down_pairs = net.both_cores(join_plane(down_way, down_got, 2))
    slope = (share + hidden * jnp.exp(-0.5 * hidden * hidden) * INV_ROOT_TAU).astype(bf16)
    down = [
        jnp.stack(
            [
                d.reshape(group, part, -1)[:, :, b * half_mid : (b + 1) * half_mid]
                for b in range(blocks)
            ],
            axis=1,
        )
        for d in down_pairs
    ]
    (down_full,) = together(jnp.concatenate(down, axis=3).reshape(wide, width))

    def start_sum(left, right):
        return dot_tn(left, net.core_half(right, True)).astype(bf16)

    def own_sum(left, right, other):
        total = dot_tn(left, net.core_half(right)) + other.astype(f32)
        total = total.astype(bf16)
        return total.reshape(2, 2, 2, -1, total.shape[1])

    def part_plane(piece):
        pairs = [net.part_with(p, name, 2) for p, name in zip(ways(piece), plane)]
        return [p[0] for p in pairs], [p[1] for p in pairs]

    def add_plane(keeps, others):
        return jnp.concatenate([add(pair) for pair in zip(keeps, others)], axis=-1)

    def exchange_plane(piece):
        done = []
        for p, name in zip(ways(piece), plane):
            for other in (net.other_way(name),) + net.extra:
                p = add((p, net.swap(p, other)))
            done.append(p)
        return done

    def grow_plane(pieces):
        return jnp.concatenate(
            [
                net.grow(p, name, 0).reshape(-1, p.shape[-1])
                for p, name in zip(pieces, plane)
            ],
            axis=1,
        )

    grad_branch = jnp.pad(out_grad, fill).reshape(row_count, width)
    grad_branch = grad_branch * live_rows.astype(bf16)
    grad_down_b = jnp.sum(grad_branch.astype(f32), axis=0, keepdims=True)
    branch_2, d_send = together(grad_branch, start_sum(active, grad_branch))
    d_other = net.swap(d_send, net.core)
    result = middle + (dot_nn(active, down_full) + down_bias)
    layer_out = (result * live_rows).astype(bf16)
    layer_out = layer_out.reshape(slot_count, padded, width)[:, :length]
    branch_3, layer_out = together(grad_branch, layer_out)
    d_piece = own_sum(active, branch_3, d_other)
    branch_2, d_piece = together(branch_2, d_piece)
    fine = d_piece.shape[3] // 2
    d_pairs = [
        net.part_with(d_piece[:, :, :, i * fine : (i + 1) * fine], name, 2)
        for i, name in enumerate(plane)
    ]
    d_keeps, d_others = [p[0] for p in d_pairs], [p[1] for p in d_pairs]
    grad_hidden, up_sums = hidden_back(branch_2, down_full, slope)
    grad_hidden, u_send = together(grad_hidden, start_sum(normed_two, grad_hidden))
    u_other = net.swap(u_send, net.core)
    grad_middle, grad_attn, mid_sums = matmul_norm_back(
        grad_hidden, up_full, middle, gain_2, grad_branch, slot_count, True
    )
    grad_attn, d_1, d_2, o_1, o_2 = together(grad_attn, *d_keeps, *d_others)
    grad_hidden, grad_attn = together(grad_hidden, grad_attn)
    grad_attn, p_send = together(grad_attn, start_sum(mixed, grad_attn))
    p_other = net.swap(p_send, net.core)
    u_piece = own_sum(normed_two, grad_hidden, u_other)
    grad_attn, u_piece = together(grad_attn, u_piece)
    p_piece = own_sum(mixed, grad_attn, p_other)
    u_piece = jnp.concatenate([u_piece, p_piece], axis=-1)
    grad_attn_2, u_piece, d_1, d_2, o_1, o_2 = together(grad_attn, u_piece, d_1, d_2, o_1, o_2)
    d_piece = add_plane([d_1, d_2], [o_1, o_2])
    d_pair = net.part_with(d_piece, near, 1)
    u_keeps, u_others = part_plane(u_piece)
    grad_mixed = dot_nt(grad_attn_2, proj_full).astype(bf16)
    grad_joined, joined_sums = attention_back(
        joined, probs, grad_mixed.reshape(slot_count, padded, width)
    )
    grad_joined, d_keep, d_other, u_1, u_2, o_1, o_2 = together(
        grad_joined.reshape(row_count, 3 * width), *d_pair, *u_keeps, *u_others
    )
    grad_joined, q_send, d_keep, d_other, u_1, u_2, o_1, o_2 = together(
        grad_joined, start_sum(normed_one, grad_joined), d_keep, d_other, u_1, u_2, o_1, o_2
    )
    q_other = net.swap(q_send, net.core)
    u_piece = add_plane([u_1, u_2], [o_1, o_2])
    d_piece = add((d_keep, d_other))
    grad_joined, d_piece, u_piece = together(grad_joined, d_piece, u_piece)
    u_pair = net.part_with(u_piece, near, 1)
    d_pair = net.part_with(d_piece, far, 0)
    q_piece = own_sum(normed_one, grad_joined, q_other)
    grad_joined, q_piece = together(grad_joined, q_piece)
    q_keeps, q_others = part_plane(q_piece)
    grad_tokens, first_sums = matmul_norm_back(
        grad_joined, qkv_full, low_inputs, gain_1, grad_middle, slot_count, False
    )
    grad_tokens = grad_tokens.reshape(slot_count, padded, width)[:, :length]

    vectors = [
        mid_sums[2:3],
        mid_sums[0:2],
        grad_down_b,
        joined_sums[:, :width],
        joined_sums[:, 2 * width :],
        first_sums[0:2],
    ]
    vectors += [up_sums[:, k * width : (k + 1) * width] for k in range(group)]
    vectors = jnp.concatenate(vectors, axis=0)

    vectors, u_keep, u_other, d_keep, d_other, q_1, q_2, o_1, o_2 = together(
        vectors, *u_pair, *d_pair, *q_keeps, *q_others
    )
    q_piece = add_plane([q_1, q_2], [o_1, o_2])
    u_piece = add((u_keep, u_other))
    q_piece, u_piece, vectors, d_keep = together(q_piece, u_piece, vectors, d_keep)
    q_pair = net.part_with(q_piece, near, 1)
    u_pair = net.part_with(u_piece, far, 0)
    sums = vectors + net.swap(vectors, net.core)
    d_piece = exchange_plane(add((d_keep, d_other)))
    q_keep, q_other, u_keep, u_other, sums, *d_piece = together(*q_pair, *u_pair, sums, *d_piece)
    q_piece = add((q_keep, q_other))
    u_piece = add((u_keep, u_other))
    q_piece, u_piece, sums, *d_piece = together(q_piece, u_piece, sums, *d_piece)
    q_pair = net.part_with(q_piece, far, 0)
    u_piece = exchange_plane(u_piece)
    down_shard = jnp.stack(
        [net.grow(p, name, 0) for p, name in zip(d_piece, plane)], axis=1
    ).reshape(-1, half_mid)
    sums = sums + net.swap(sums, net.x)
    q_keep, q_other, sums, down_shard, *u_piece = together(*q_pair, sums, down_shard, *u_piece)
    q_1, q_2 = exchange_plane(add((q_keep, q_other)))
    up_shard = grow_plane(u_piece)
    down_pair = net.both_cores(down_shard)
    sums = sums + net.swap(sums, net.y)
    grad_down_w = jnp.concatenate(down_pair, axis=1).astype(f32)
    q_1, q_2, sums, up_shard, grad_down_w = together(q_1, q_2, sums, up_shard, grad_down_w)
    q_piece = grow_plane([q_1, q_2])
    up_pair = net.both_cores(up_shard)
    sums = sums + net.swap(sums, far)
    q_piece, sums, *up_pair = together(q_piece, sums, *up_pair)
    q_pair = net.both_cores(q_piece)
    for name in (near,) + net.extra:
        sums = sums + net.swap(sums, name)
    me = net.place_in_group()
    owned = lax.dynamic_slice_in_dim(sums[:8], me * part, part, 1)
    owned_up = lax.dynamic_index_in_dim(sums, 8 + me, 0, keepdims=False)
    grad_up_w = jnp.concatenate([p[:, :half_up] for p in up_pair], axis=1).astype(f32)
    grad_proj_w = jnp.concatenate([p[:, half_up:] for p in up_pair], axis=1).astype(f32)
    grad_qkv_w = jnp.concatenate(q_pair, axis=1).astype(f32)
    return (
        layer_out,
        grad_tokens,
        grad_qkv_w,
        owned[4],
        owned[5],
        grad_proj_w,
        owned[0],
        owned[6],
        owned[7],
        owned[1],
        owned[2],
        grad_up_w,
        owned_up,
        grad_down_w,
        owned[3],
    )


def solution(mesh):
    rep, shard = mesh.shape["rep"], mesh.shape["shard"]
    rep_bits = tuple(f"r{i}" for i in range(rep.bit_length() - 1))
    shard_bits = tuple(f"s{i}" for i in range(shard.bit_length() - 1))
    fine = Mesh(mesh.devices.reshape((2,) * (len(rep_bits) + len(shard_bits))), rep_bits + shard_bits)
    every = P(rep_bits + shard_bits, None, None)
    matrix = P(shard_bits, None)
    vector = P(shard_bits)
    return jax.shard_map(
        functools.partial(per_device, rep_bits, shard_bits),
        mesh=fine,
        in_specs=(
            every,
            P(rep_bits + shard_bits),
            matrix,
            vector,
            vector,
            matrix,
            vector,
            vector,
            vector,
            vector,
            vector,
            matrix,
            vector,
            matrix,
            vector,
            every,
        ),
        out_specs=(
            every,
            every,
            matrix,
            vector,
            vector,
            matrix,
            vector,
            vector,
            vector,
            vector,
            vector,
            matrix,
            vector,
            matrix,
            vector,
        ),
        check_vma=False,
    )
```
